32 devices in a mesh: groups: 2 (over x), dp: 4 (over y, core), tensor: 4 (over z).
Axes of the slice: x: 2, y: 2, z: 4, core: 2. Of those that a mesh axis runs over, the one named last changes fastest.
Arguments:
- input_rows: bfloat16 [8192, 8192], P(('groups', 'dp'), 'tensor'), parts along dimension 0, may hold values from -6 to 6
- key_value_weight: bfloat16 [8192, 2, 1024], P(None, None, 'tensor'), may hold values from -0.0625 to 0.0625
- adapter_down_weight: bfloat16 [64, 8192, 128], P('dp', 'tensor'), may hold values from -0.0625 to 0.0625
- adapter_up_weight: bfloat16 [64, 2, 64, 1024], P('dp', None, None, 'tensor'), may hold values from -0.75 to 0.75
- tile_page_index: int32 [64], P('groups'), parts along dimension 0, may hold values from 0 to 63, as said below
- tile_live_rows: int32 [64], P(('groups', 'dp')), parts along dimension 0, may hold values from 1 to 128, as said below
Outputs:
- kv_out: bfloat16 [8192, 2, 1024], P(('groups', 'dp'), None, 'tensor'), parts along dimension 0
The draws below stay inside these ranges and needn't reach their ends.
There are 2 independent parts, one for each index of `groups`. The reference program is written for one: setup_inputs(seed, part) draws one part's arguments, and reference() takes and returns one part's arrays. A program takes and returns all parts, laid end to end along the dimension named above; an argument that names none is the same for every part. Nothing has to cross between parts.
Inputs may be any that keep to these rules, and one draw needn't show every extreme that they name: `tile_page_index`: page p belongs to index p // 16 of dp. Among the tiles of one index of dp, at most 4 name pages of one owner, and one owner is named by exactly 4 tiles of every index of dp. `tile_live_rows`: every index of dp has a tile with 128 live rows.
All inputs are finite; a program needn't handle non-finite values.
Results may differ from the reference program's by a relative error of at most 0.0042.
Values may be sent and summed in bfloat16 or wider, within the bound.
No kernel may reach another device: no remote copies, remote signals or barrier semaphores. Data moves between devices by JAX's collectives and lax.ppermute only.
A program may use at most 192 MiB of HBM per device.

```python
import jax
import jax.numpy as jnp
from jax import lax

MODEL_WIDTH = 8192
KEY_VALUE_HEADS = 8
HEAD_SIZE = 128
ADAPTER_RANK = 64
TILE = 128
TILES_DEV = 8
ADP_DEV = 16
CAP = 4
ROWS = 4096
TILES_ALL = 32
ADAPTER_PAGES = 64


def draw_tile_page_index(key, part):
    key = jax.random.fold_in(key, 11)
    owner_count = TILES_ALL // TILES_DEV
    hot_key, rest_key = jax.random.split(key)
    hot_owner = jax.random.randint(hot_key, (), 0, owner_count)
    others = (hot_owner + 1 + jnp.arange(owner_count - 1, dtype=jnp.int32)) % owner_count
    owner_pool = jnp.repeat(others, CAP)

    def one_device(device_key):
        first_key, second_key, third_key = jax.random.split(device_key, 3)
        picked = jax.random.permutation(first_key, owner_pool)[:TILES_DEV - CAP]
        owners = jnp.concatenate([jnp.full((CAP,), hot_owner, jnp.int32), picked.astype(jnp.int32)])
        owners = jax.random.permutation(second_key, owners)
        slot_ids = jax.random.randint(third_key, (TILES_DEV,), 0, ADP_DEV)
        return owners * ADP_DEV + slot_ids
    device_keys = jax.random.split(rest_key, owner_count)
    return jax.vmap(one_device)(device_keys).reshape(-1).astype(jnp.int32)


def draw_tile_live_rows(key, part):
    key = jax.random.fold_in(key, 23)
    first_key, second_key = jax.random.split(key)
    owner_count = TILES_ALL // TILES_DEV
    live_rows = jax.random.randint(first_key, (TILES_ALL,), 1, TILE + 1)
    full_at = jax.random.randint(second_key, (owner_count,), 0, TILES_DEV)
    position = jnp.arange(TILES_ALL, dtype=jnp.int32) % TILES_DEV
    device = jnp.arange(TILES_ALL, dtype=jnp.int32) // TILES_DEV
    return jnp.where(position == full_at[device], TILE, live_rows).astype(jnp.int32)


def level_of(rng, dims, cuts, least, top_value):
    loudness = 1.0
    for dim, blocks in cuts:
        draws = jax.random.uniform(jax.random.fold_in(jax.random.fold_in(rng, 6), dim), (blocks,), jnp.float32, least / len(cuts), top_value / len(cuts))
        loudness = loudness * jnp.repeat(jnp.exp(draws), dims[dim] // blocks).reshape((-1,) + (1,) * (len(dims) - 1 - dim))
    return loudness


def normal_values(key, dims, deviation, reach, cuts=(), kind=jnp.bfloat16):
    drawn = deviation * jax.random.normal(key, dims, jnp.float32)
    if cuts:
        drawn = drawn * level_of(key, dims, cuts, -0.22, 0.18)
    return jnp.clip(drawn, -reach, reach).astype(kind)


def setup_inputs(seed: int = 0, part: int = 0) -> dict:
    streams_of = jax.random.split(jax.random.key(seed), 7)
    part_keys = jax.random.split(jax.random.fold_in(streams_of[6], part), 7)
    input_rows = normal_values(part_keys[0], (ROWS, MODEL_WIDTH), 1.0, 6.0, ((0, 4), (1, 4)))
    key_value_weight = normal_values(streams_of[1], (MODEL_WIDTH, 2, KEY_VALUE_HEADS * HEAD_SIZE), MODEL_WIDTH ** -0.5, 0.0625, ((2, 4),))
    adapter_down_weight = normal_values(streams_of[2], (ADAPTER_PAGES, MODEL_WIDTH, 2 * ADAPTER_RANK), MODEL_WIDTH ** -0.5, 0.0625, ((0, 4), (1, 4)))
    adapter_up_weight = normal_values(streams_of[3], (ADAPTER_PAGES, 2, ADAPTER_RANK, KEY_VALUE_HEADS * HEAD_SIZE), ADAPTER_RANK ** -0.5, 0.75, ((0, 4), (3, 4)))
    tile_page_index = draw_tile_page_index(jax.random.fold_in(jax.random.fold_in(streams_of[6], part), 71), part)
    tile_live_rows = draw_tile_live_rows(jax.random.fold_in(jax.random.fold_in(streams_of[6], part), 71), part)
    return dict(input_rows=input_rows, key_value_weight=key_value_weight, adapter_down_weight=adapter_down_weight, adapter_up_weight=adapter_up_weight, tile_page_index=tile_page_index, tile_live_rows=tile_live_rows)


def reference(input_rows, key_value_weight, adapter_down_weight, adapter_up_weight, tile_page_index, tile_live_rows):
    total_rows = input_rows.shape[0]
    base_part = jnp.dot(input_rows, key_value_weight.reshape(MODEL_WIDTH, 2 * KEY_VALUE_HEADS * HEAD_SIZE), preferred_element_type=jnp.float32)
    base_part = base_part.reshape(total_rows, 2, KEY_VALUE_HEADS * HEAD_SIZE)
    blocks = input_rows.reshape(TILES_ALL, TILE, MODEL_WIDTH)

    def one_tile(entry):
        tile_block, page_index = entry
        down_matrix = lax.dynamic_index_in_dim(adapter_down_weight, page_index, 0, keepdims=False)
        up_matrix = lax.dynamic_index_in_dim(adapter_up_weight, page_index, 0, keepdims=False)
        reduced_projection = jnp.dot(tile_block, down_matrix, preferred_element_type=jnp.float32).astype(jnp.bfloat16)
        key_part = jnp.dot(reduced_projection[:, :ADAPTER_RANK], up_matrix[0], preferred_element_type=jnp.float32)
        value_part = jnp.dot(reduced_projection[:, ADAPTER_RANK:], up_matrix[1], preferred_element_type=jnp.float32)
        return jnp.stack([key_part, value_part], axis=1)

    expand = lax.map(one_tile, (blocks, tile_page_index.astype(jnp.int32)))
    expand = expand.reshape(total_rows, 2, KEY_VALUE_HEADS * HEAD_SIZE)
    live_mask = (jnp.arange(TILE, dtype=jnp.int32)[None, :] < tile_live_rows[:, None]).reshape(total_rows)
    summed = base_part + expand
    return jnp.where(live_mask[:, None, None], summed, jnp.zeros_like(summed)).astype(jnp.bfloat16)
```

```python
import functools

import jax
import jax.numpy as jnp
from jax import lax
from jax.experimental import pallas as pl
from jax.experimental.pallas import tpu as pltpu
from jax.sharding import PartitionSpec as P


def flip(x, axis, size, mask):
    return lax.ppermute(x, axis, [(i, i ^ mask) for i in range(size)])


def bits(size, first=1):
    out = []
    while first < size:
        out.append(first)
        first *= 2
    return out


def shrink_kernel(kind, own_at, mate_at, near_at, far_at, x, own, mate, near, far, out):
    t = pl.program_id(0)
    for which, pages in enumerate((own, mate, near, far)):

        @pl.when(kind[t] == which)
        def _(pages=pages):
            out[...] = jnp.dot(
                x[...], pages[0], preferred_element_type=jnp.float32
            ).astype(out.dtype)


def tile_shrink(kind, places, rows, pools, tiles):
    tile_rows = rows.shape[0] // tiles
    features = rows.shape[1]
    columns = pools[0].shape[2]
    held = []
    for which in range(4):
        used = kind == which
        last = lax.cummax(jnp.where(used, jnp.arange(tiles, dtype=jnp.int32), 0))
        held.append(jnp.where(used, places, 0)[last])

    def pool_spec(which):
        return pl.BlockSpec((1, features, columns), lambda t, *s: (s[1 + which][t], 0, 0))

    return pl.pallas_call(
        shrink_kernel,
        out_shape=jax.ShapeDtypeStruct((rows.shape[0], columns), jnp.bfloat16),
        grid_spec=pltpu.PrefetchScalarGridSpec(
            num_scalar_prefetch=5,
            grid=(tiles,),
            in_specs=[pl.BlockSpec((tile_rows, features), lambda t, *s: (t, 0))]
            + [pool_spec(which) for which in range(4)],
            out_specs=pl.BlockSpec((tile_rows, columns), lambda t, *s: (t, 0)),
        ),
        compiler_params=pltpu.CompilerParams(vmem_limit_bytes=32 << 20),
    )(kind, *held, rows, *pools)


def on_device(
    input_rows,
    key_value_weight,
    adapter_down_weight,
    adapter_up_weight,
    tile_page_index,
    tile_live_rows,
):
    groups = lax.axis_size("groups")
    ranks = lax.axis_size("dp")
    shares = lax.axis_size("tensor")
    group = lax.axis_index("groups")
    rank = lax.axis_index("dp")
    share = lax.axis_index("tensor")
    chips = ranks // 2
    chip, core = rank // 2, rank % 2
    tiles = tile_live_rows.shape[0]
    local_pages = adapter_down_weight.shape[0]
    chip_pages = 2 * local_pages
    capacity = max(2, (2 * tiles + ranks - 1) // ranks)
    slots = 2 * capacity
    rows, features = input_rows.shape
    tile_rows = rows // tiles
    column_width = key_value_weight.shape[2]
    columns = 2 * column_width
    half = adapter_down_weight.shape[2] // 2

    table = tile_page_index.reshape(chips, 2 * tiles)
    page_range = jnp.arange(ranks * local_pages, dtype=jnp.int32)
    need = jnp.any(table[:, :, None] == page_range[None, None, :], axis=1)
    need = need.reshape(chips, chips, chip_pages)
    position = jnp.cumsum(need.astype(jnp.int32), axis=2) - 1
    chip_range = jnp.arange(chip_pages, dtype=jnp.int32)
    slot_range = jnp.arange(2 * slots, dtype=jnp.int32)
    near_down, near_up, far_down, far_up = [], [], [], []
    for offset in range(1, chips):
        wanted = need[chip ^ offset, chip]
        place = position[chip ^ offset, chip]
        listed = jnp.sum(
            jnp.where(wanted[None, :] & (place[None, :] == slot_range[:, None]), chip_range[None, :], 0),
            axis=1,
        ).reshape(2, slots)
        here = listed[core]
        there = listed[1 - core]
        mine = (here // local_pages) == core
        down = adapter_down_weight[here % local_pages]
        up = adapter_up_weight[here % local_pages]
        other_down = flip(adapter_down_weight[there % local_pages], "dp", ranks, 1)
        other_up = flip(adapter_up_weight[there % local_pages], "dp", ranks, 1)
        down = jnp.where(mine[:, None, None], down, other_down)
        up = jnp.where(mine[:, None, None, None], up, other_up)
        down = flip(down, "dp", ranks, 2 * offset)
        up = flip(up, "dp", ranks, 2 * offset)
        near_down.append(down)
        near_up.append(up)
        far_down.append(flip(down, "dp", ranks, 1))
        far_up.append(flip(up, "dp", ranks, 1))
    near_down, far_down = jnp.concatenate(near_down), jnp.concatenate(far_down)
    near_up, far_up = jnp.concatenate(near_up), jnp.concatenate(far_up)

    rank_table = tile_page_index.reshape(ranks, tiles)
    mate_pages = rank_table[rank ^ 1]
    asked = (mate_pages // local_pages) == rank
    order = jnp.cumsum(asked.astype(jnp.int32)) - 1
    outgoing = jnp.sum(
        jnp.where(
            asked[None, :] & (order[None, :] == jnp.arange(capacity, dtype=jnp.int32)[:, None]),
            (mate_pages % local_pages)[None, :],
            0,
        ),
        axis=1,
    )
    mate_down = flip(adapter_down_weight[outgoing], "dp", ranks, 1)
    mate_up = flip(adapter_up_weight[outgoing], "dp", ranks, 1)

    pages = rank_table[rank]
    owner = pages // local_pages
    from_mate = owner == (rank ^ 1)
    mate_order = jnp.cumsum(from_mate.astype(jnp.int32)) - 1
    owner_chip = owner // 2
    slot = position[chip, owner_chip, pages % chip_pages]
    sender = slot // slots
    cross_at = ((owner_chip ^ chip) - 1) * slots + slot % slots
    kind = jnp.where(
        owner == rank, 0, jnp.where(from_mate, 1, jnp.where(sender == core, 2, 3))
    ).astype(jnp.int32)
    places = jnp.where(
        owner == rank, pages % local_pages, jnp.where(from_mate, mate_order, cross_at)
    ).astype(jnp.int32)

    plane = groups * ranks
    spot = group * ranks + rank
    part = features // plane
    masks = [0]
    steps = [("dp", ranks, m, m) for m in bits(ranks, 2)]
    steps += [("groups", groups, m, m * ranks) for m in bits(groups)]
    steps += [("dp", ranks, 1, 1)]
    for _, _, _, m in steps:
        masks = masks + [m ^ other for other in masks]
    weights = {}
    for k in range(1, shares):
        start = (share ^ k) * features + spot * part
        piece = lax.dynamic_slice_in_dim(key_value_weight, start, part, 0).reshape(part, columns)
        weights[k] = flip(piece, "tensor", shares, k)
    for k in range(1, shares):
        for axis, size, m, _ in steps:
            weights[k] = jnp.concatenate([weights[k], flip(weights[k], axis, size, m)])
    own_weight = lax.dynamic_slice_in_dim(key_value_weight, share * features, features, 0)
    own_weight = own_weight.reshape(features, columns)
    turned = jnp.concatenate(
        [lax.dynamic_slice_in_dim(input_rows, (spot ^ m) * part, part, 1) for m in masks], axis=1
    )

    chunks = 2
    chunk_rows = rows // chunks
    totals = []
    for i in range(chunks):
        cut = lax.slice_in_dim(turned, i * chunk_rows, (i + 1) * chunk_rows, axis=0)
        straight = lax.slice_in_dim(input_rows, i * chunk_rows, (i + 1) * chunk_rows, axis=0)
        sums = {
            k: jnp.dot(cut, weights[k], preferred_element_type=jnp.float32) for k in range(1, shares)
        }
        sums[0] = jnp.dot(straight, own_weight, preferred_element_type=jnp.float32)
        for m in bits(shares):
            leaving = [k for k in sums if k & m]
            arrived = {k: flip(sums.pop(k).astype(jnp.bfloat16), "tensor", shares, m) for k in leaving}
            for k, value in arrived.items():
                sums[k ^ m] = sums[k ^ m] + value.astype(jnp.float32)
        totals.append(sums[0])
    base = jnp.concatenate(totals)

    shrink = tile_shrink(
        kind, places, input_rows, (adapter_down_weight, mate_down, near_down, far_down), tiles
    )
    shrink_sum = shrink.astype(jnp.float32)
    for m in bits(shares):
        sent = shrink_sum.astype(jnp.bfloat16)
        shrink_sum = shrink_sum + flip(sent, "tensor", shares, m).astype(jnp.float32)
    reduced = shrink_sum.astype(jnp.bfloat16).reshape(tiles, tile_rows, 2 * half)
    sizes = (local_pages, capacity, near_up.shape[0], far_up.shape[0])
    firsts = jnp.array([sum(sizes[:i]) for i in range(4)], jnp.int32)
    up_pool = jnp.concatenate([adapter_up_weight, mate_up, near_up, far_up])
    tile_up = up_pool[firsts[kind] + places]
    expand = [
        jnp.einsum(
            "trk,tkc->trc",
            reduced[..., which * half : (which + 1) * half],
            tile_up[:, which],
            preferred_element_type=jnp.float32,
        )
        for which in range(2)
    ]
    expand = jnp.stack(expand, axis=2).reshape(rows, 2, column_width)
    live = (jnp.arange(tile_rows, dtype=jnp.int32)[None, :] < tile_live_rows[:, None]).reshape(rows)
    summed = base.reshape(rows, 2, column_width) + expand
    return jnp.where(live[:, None, None], summed, jnp.zeros_like(summed)).astype(jnp.bfloat16)


def solution(mesh):
    return jax.shard_map(
        on_device,
        mesh=mesh,
        in_specs=(
            P(("groups", "dp"), "tensor"),
            P(None, None, "tensor"),
            P("dp", "tensor", None),
            P("dp", None, None, "tensor"),
            P("groups"),
            P(("groups", "dp")),
        ),
        out_specs=P(("groups", "dp"), None, "tensor"),
        check_vma=False,
    )
```

```python
import functools

import jax
import jax.numpy as jnp
from jax import lax
from jax.experimental import pallas as pl
from jax.experimental.pallas import tpu as pltpu
from jax.sharding import PartitionSpec as P


def flip(x, axis, size, mask):
    return lax.ppermute(x, axis, [(i, i ^ mask) for i in range(size)])


def bits(size, first=1):
    out = []
    while first < size:
        out.append(first)
        first *= 2
    return out


def after(value, *others):
    return lax.optimization_barrier((value,) + others)[0]


def pick_kernel(low, own_at, mate_at, mine, own, mate, out):
    j = low + pl.program_id(0)

    @pl.when(mine[j] == 1)
    def _():
        out[...] = own[...]

    @pl.when(mine[j] != 1)
    def _():
        out[...] = mate[...]


def pick_pages(lists, low, count, own, mate):
    block = (1,) + own.shape[1:]
    return pl.pallas_call(
        functools.partial(pick_kernel, low),
        out_shape=jax.ShapeDtypeStruct((count,) + block[1:], own.dtype),
        grid_spec=pltpu.PrefetchScalarGridSpec(
            num_scalar_prefetch=3,
            grid=(count,),
            in_specs=[
                pl.BlockSpec(block, lambda j, own_at, mate_at, mine: (own_at[low + j], 0, 0)),
                pl.BlockSpec(block, lambda j, own_at, mate_at, mine: (mate_at[low + j], 0, 0)),
            ],
            out_specs=pl.BlockSpec(block, lambda j, own_at, mate_at, mine: (j, 0, 0)),
        ),
    )(*lists, own, mate)


def side_kernel(at, weight, out):
    width = weight.shape[2]
    for which in range(2):
        out[0, :, which * width : (which + 1) * width] = weight[:, which, :]


def side_by_side(at, weight, part, low, count):
    _, two, width = weight.shape
    return pl.pallas_call(
        side_kernel,
        out_shape=jax.ShapeDtypeStruct((count, part, two * width), weight.dtype),
        grid_spec=pltpu.PrefetchScalarGridSpec(
            num_scalar_prefetch=1,
            grid=(count,),
            in_specs=[pl.BlockSpec((part, two, width), lambda j, at: (at[low + j], 0, 0))],
            out_specs=pl.BlockSpec((1, part, two * width), lambda j, at: (j, 0, 0)),
        ),
    )(at, weight)


def shrink_kernel(pools, kind, *refs):
    x, out = refs[pools], refs[-1]
    t = pl.program_id(0)
    for number, pages in enumerate(refs[pools + 1 : -1]):

        @pl.when(kind[t] == number)
        def _(pages=pages):
            out[...] = jnp.dot(x[...], pages[0], preferred_element_type=jnp.float32).astype(out.dtype)


def tile_shrink(kind, places, rows, pools, tiles):
    tile_rows = rows.shape[0] // tiles
    features = rows.shape[1]
    columns = pools[0].shape[2]
    numbers = jnp.arange(len(pools), dtype=jnp.int32)
    used = kind[None, :] == numbers[:, None]
    last = lax.cummax(jnp.where(used, jnp.arange(tiles, dtype=jnp.int32)[None, :], 0), axis=1)
    same = last[:, :, None] == jnp.arange(tiles, dtype=jnp.int32)[None, None, :]
    held = jnp.sum(jnp.where(same & used[:, None, :], places[None, None, :], 0), axis=2)

    def pool_spec(number):
        return pl.BlockSpec((1, features, columns), lambda t, *s: (s[1 + number][t], 0, 0))

    return pl.pallas_call(
        functools.partial(shrink_kernel, len(pools)),
        out_shape=jax.ShapeDtypeStruct((rows.shape[0], columns), jnp.bfloat16),
        grid_spec=pltpu.PrefetchScalarGridSpec(
            num_scalar_prefetch=1 + len(pools),
            grid=(tiles,),
            in_specs=[pl.BlockSpec((tile_rows, features), lambda t, *s: (t, 0))]
            + [pool_spec(number) for number in range(len(pools))],
            out_specs=pl.BlockSpec((tile_rows, columns), lambda t, *s: (t, 0)),
        ),
        compiler_params=pltpu.CompilerParams(vmem_limit_bytes=48 << 20),
    )(kind, *[held[number] for number in range(len(pools))], rows, *pools)


def finish_kernel(offsets, live, up_at, *refs):
    keys, values, more_keys, more_values, reduced, up, out, held = refs
    t = pl.program_id(0)
    tile_rows, two, width = out.shape
    half = up.shape[2]
    room, rest = keys.shape[0], more_keys.shape[0]

    @pl.when(t == 0)
    def _():
        for which, (first, second) in enumerate(((keys, more_keys), (values, more_values))):
            held[which, :room] = first[...]
            held[which, room : room + rest] = second[...]
            held[which, room + rest :] = jnp.zeros((tile_rows, width), jnp.float32)

    low = pl.multiple_of((offsets[t] // 8) * 8, 8)
    shift = offsets[t] % 8
    alive = lax.broadcasted_iota(jnp.int32, (tile_rows, width), 0) < live[t]
    for which in range(2):
        expand = jnp.dot(
            reduced[:, which * half : (which + 1) * half],
            up[0, which],
            preferred_element_type=jnp.float32,
        )
        wide = held[which, pl.ds(low, tile_rows + 8), :]
        base = pltpu.roll(wide, tile_rows + 8 - shift, 0)[:tile_rows]
        out[:, which, :] = jnp.where(alive, base + expand, 0.0).astype(out.dtype)


def finish(offsets, live, up_at, totals, rest, reduced, ups):
    tiles = offsets.shape[0]
    rows, columns = reduced.shape
    tile_rows = rows // tiles
    width = totals[0].shape[1]

    def whole(array):
        return pl.BlockSpec(array.shape, lambda t, *s: (0, 0))

    return pl.pallas_call(
        finish_kernel,
        out_shape=jax.ShapeDtypeStruct((rows, 2, width), jnp.bfloat16),
        grid_spec=pltpu.PrefetchScalarGridSpec(
            num_scalar_prefetch=3,
            grid=(tiles,),
            in_specs=[whole(array) for array in (*totals, *rest)]
            + [
                pl.BlockSpec((tile_rows, columns), lambda t, *s: (t, 0)),
                pl.BlockSpec((1,) + ups.shape[1:], lambda t, *s: (s[2][t], 0, 0, 0)),
            ],
            out_specs=pl.BlockSpec((tile_rows, 2, width), lambda t, *s: (t, 0, 0)),
            scratch_shapes=[pltpu.VMEM((2, rows + tile_rows, width), jnp.float32)],
        ),
        compiler_params=pltpu.CompilerParams(vmem_limit_bytes=48 << 20),
    )(offsets, live, up_at, *totals, *rest, reduced, ups)


def on_device(
    input_rows,
    key_value_weight,
    adapter_down_weight,
    adapter_up_weight,
    tile_page_index,
    tile_live_rows,
):
    groups = lax.axis_size("groups")
    ranks = lax.axis_size("dp")
    shares = lax.axis_size("tensor")
    group = lax.axis_index("groups")
    rank = lax.axis_index("dp")
    share = lax.axis_index("tensor")
    chips = ranks // 2
    chip, core = rank // 2, rank % 2
    tiles = tile_live_rows.shape[0]
    local_pages = adapter_down_weight.shape[0]
    chip_pages = 2 * local_pages
    capacity = max(2, (2 * tiles + ranks - 1) // ranks)
    most_slots = 2 * capacity
    rows, features = input_rows.shape
    tile_rows = rows // tiles
    column_width = key_value_weight.shape[2]
    half = adapter_down_weight.shape[2] // 2

    columns = 2 * column_width
    plane = groups * ranks
    part = features // plane

    mate_down = flip(adapter_down_weight, "dp", ranks, 1)
    mate_up = flip(adapter_up_weight, "dp", ranks, 1)

    steps = [("dp", ranks, m, (rank // m) % 2) for m in bits(ranks, 2)]
    steps += [("groups", groups, m, (group // m) % 2) for m in bits(groups)]
    steps += [("dp", ranks, 1, core)]
    over_chips = len(bits(ranks, 2))
    spot = sum(bit << i for i, (_, _, _, bit) in enumerate(steps))
    turns = list(range(shares - 1, 0, -1))
    starts = (share ^ jnp.array(turns, jnp.int32)) * plane + spot
    piece = side_by_side(starts, key_value_weight, part, 0, 1)[0]
    weights = {}
    for which in range(2):
        cut = piece[:, which * column_width : (which + 1) * column_width]
        weights[turns[0], which] = flip(cut, "tensor", shares, turns[0])
    for i, k in enumerate(turns[1:]):
        piece = side_by_side(starts, key_value_weight, part, 1 + i, 1)[0]
        weights[k, 2] = flip(piece, "tensor", shares, k)

    table = tile_page_index.reshape(chips, 2 * tiles)
    page_range = jnp.arange(ranks * local_pages, dtype=jnp.int32)
    need = jnp.any(table[:, :, None] == page_range[None, None, :], axis=1)
    need = need.reshape(chips, chips, chip_pages)
    position = jnp.cumsum(need.astype(jnp.int32), axis=2) - 1
    usual = -(-5 * most_slots // 8)
    more = -(-6 * most_slots // 8)
    cuts = [0, max(1, usual // 5), max(2, 3 * usual // 5), usual]
    firsts = [0, 2 * usual, 2 * more, 2 * most_slots]
    most_pages = jnp.max(
        jnp.where(jnp.eye(chips, dtype=jnp.bool_), 0, position[:, :, -1] + 1)
    )
    slot_range = jnp.arange(2 * most_slots, dtype=jnp.int32)
    chip_range = jnp.arange(chip_pages, dtype=jnp.int32)

    offsets = jnp.cumsum(tile_live_rows) - tile_live_rows
    live_total = jnp.sum(tile_live_rows)
    live = jnp.arange(tile_rows, dtype=jnp.int32)[None, :] < tile_live_rows[:, None]
    packed_place = offsets[:, None] + jnp.arange(tile_rows, dtype=jnp.int32)[None, :]
    packed_place = jnp.where(live, packed_place, -1).reshape(rows)
    room = -(-13 * rows // 256) * 16

    def pack(first, last, x):
        pick = packed_place[None, :] == jnp.arange(first, last, dtype=jnp.int32)[:, None]
        return jnp.dot(pick.astype(x.dtype), x, preferred_element_type=jnp.float32).astype(x.dtype)

    past = []

    def cross(value, axis, size, m):
        if len(past) > 1:
            value = after(value, past[-2])
        past.append(flip(value, axis, size, m))
        return past[-1]

    def spread(held, first, last):
        for i in range(first, last):
            axis, size, m, bit = steps[i]
            got = cross(held, axis, size, m) if i < over_chips else flip(held, axis, size, m)
            held = jnp.concatenate([jnp.where(bit == 1, got, held), jnp.where(bit == 1, held, got)])
        return held

    keys = list(weights)
    for key in keys[:2]:
        weights[key] = spread(weights[key], 0, over_chips)

    listed = []
    for offset in range(1, chips):
        wanted = need[chip ^ offset, chip]
        place = position[chip ^ offset, chip]
        listed.append(
            jnp.sum(
                jnp.where(
                    wanted[None, :] & (place[None, :] == slot_range[:, None]), chip_range[None, :], 0
                ),
                axis=1,
            )
        )
    up_pool = jnp.where(core == 0, adapter_up_weight, mate_up), jnp.where(core == 0, mate_up, adapter_up_weight)
    up_pool = jnp.concatenate(up_pool)

    sent_lists = []
    for offset in range(1, chips):
        halves = [
            listed[offset - 1][low:high].reshape(2, (high - low) // 2)
            for low, high in zip(firsts[:-1], firsts[1:])
        ]
        halves = jnp.concatenate(halves, axis=1)
        sent = jnp.where(core == 0, halves[0], halves[1])
        mine = ((sent // local_pages) == core).astype(jnp.int32)
        at = sent % local_pages
        sent_lists.append((sent, (at * mine, at * (1 - mine), mine)))

    picked = {}
    for offset in range(1, chips):
        for i in range(3):
            picked[offset, i] = pick_pages(
                sent_lists[offset - 1][1],
                cuts[i],
                cuts[i + 1] - cuts[i],
                adapter_down_weight,
                mate_down,
            )
    pools = [adapter_down_weight, mate_down]
    pool_of = {}

    def send_pages(offset, i):
        got = cross(picked[offset, i], "dp", ranks, 2 * offset)
        pool_of[offset, i] = len(pools)
        pools.extend([got, flip(got, "dp", ranks, 1)])

    for offset in range(1, chips):
        send_pages(offset, 0)
    for key in keys[2:]:
        weights[key] = spread(weights[key], 0, over_chips)
    for offset in range(1, chips):
        send_pages(offset, 1)
        send_pages(offset, 2)
    near_ups = [
        cross(up_pool[sent_lists[offset - 1][0][:usual]], "dp", ranks, 2 * offset)
        for offset in range(1, chips)
    ]
    near_up = jnp.concatenate(near_ups)
    up_pools = [up_pool, near_up, flip(near_up, "dp", ranks, 1)]

    for key in keys:
        weights[key] = spread(weights[key], over_chips, len(steps))
    def weight_of(weights, k, which):
        if (k, which) in weights:
            return weights[k, which]
        return weights[k, 2][:, which * column_width : (which + 1) * column_width]

    def own_weight(weight):
        at = share * plane + jnp.arange(plane, dtype=jnp.int32)
        return side_by_side(at, weight, part, 0, plane).reshape(features, columns)

    def project(packed, weights, own=None):
        sums = {}
        for k in turns:
            for which in range(2):
                sums[k, which] = jnp.dot(
                    packed, weight_of(weights, k, which), preferred_element_type=jnp.float32
                )
            if k == turns[0] and own is None:
                sent = [sums[k, which].astype(jnp.bfloat16) for which in range(2)]
                own = own_weight(after(key_value_weight, *sent))
        for which in range(2):
            sums[0, which] = jnp.dot(
                packed,
                own[:, which * column_width : (which + 1) * column_width],
                preferred_element_type=jnp.float32,
            )
        for m in bits(shares):
            arrived = {
                (k, which): flip(sums.pop((k, which)).astype(jnp.bfloat16), "tensor", shares, m)
                for k in turns
                for which in range(2)
                if (k, which) in sums and k & m
            }
            for (k, which), value in arrived.items():
                sums[k ^ m, which] = sums[k ^ m, which] + value.astype(jnp.float32)
        return [sums[0, which] for which in range(2)], own

    packed = pack(0, room, after(input_rows, *picked.values()))
    totals, own = project(packed, weights)
    rest = lax.cond(
        live_total > room,
        lambda operands: project(pack(room, rows, operands[0]), *operands[1:])[0],
        lambda operands: [jnp.zeros((rows - room, column_width), jnp.float32)] * 2,
        (input_rows, weights, own),
    )

    for stage in (1, 2):

        def send_more(sources):
            own_down, other_down, ups = sources
            got = []
            for offset in range(1, chips):
                low, count = firsts[stage] // 2, (firsts[stage + 1] - firsts[stage]) // 2
                numbers, lists = sent_lists[offset - 1]
                send = numbers[low : low + count]
                down = pick_pages(lists, low, count, own_down, other_down)
                got.append((flip(down, "dp", ranks, 2 * offset), flip(ups[send], "dp", ranks, 2 * offset)))
            down = jnp.concatenate([pair[0] for pair in got])
            up = jnp.concatenate([pair[1] for pair in got])
            return down, flip(down, "dp", ranks, 1), up, flip(up, "dp", ranks, 1)

        def send_none(sources):
            own_down, other_down, ups = sources
            count = (chips - 1) * (firsts[stage + 1] - firsts[stage]) // 2
            down = jnp.zeros((count,) + own_down.shape[1:], own_down.dtype)
            up = jnp.zeros((count,) + ups.shape[1:], ups.dtype)
            return down, down, up, up

        if firsts[stage + 1] > firsts[stage]:
            near, far, near_up, far_up = lax.cond(
                most_pages > firsts[stage],
                send_more,
                send_none,
                (adapter_down_weight, mate_down, up_pool),
            )
            pool_of[stage] = len(pools)
            pools += [near, far]
            up_pools += [near_up, far_up]

    pages = tile_page_index.reshape(ranks, tiles)[rank]
    owner = pages // local_pages
    owner_chip = owner // 2
    step = owner_chip ^ chip
    entry = position[chip, owner_chip, pages % chip_pages]
    kind = jnp.where(owner == rank, 0, 1)
    places = pages % local_pages
    up_at = pages % chip_pages
    up_first = up_pool.shape[0]
    for stage in range(3):
        count = (firsts[stage + 1] - firsts[stage]) // 2
        if count == 0:
            continue
        here = (owner_chip != chip) & (entry >= firsts[stage])
        sender, at = (entry - firsts[stage]) // count, (entry - firsts[stage]) % count
        far = (sender != core).astype(jnp.int32)
        up_at = jnp.where(here, up_first + (far * (chips - 1) + step - 1) * count + at, up_at)
        up_first += 2 * (chips - 1) * count
        if stage:
            kind = jnp.where(here, pool_of[stage] + far, kind)
            places = jnp.where(here, (step - 1) * count + at, places)
            continue
        for offset in range(1, chips):
            for i in range(3):
                chosen = here & (step == offset) & (at >= cuts[i])
                kind = jnp.where(chosen, pool_of[offset, i] + far, kind)
                places = jnp.where(chosen, at - cuts[i], places)

    shrink = tile_shrink(
        kind.astype(jnp.int32), places.astype(jnp.int32), input_rows, pools, tiles
    ).astype(jnp.float32)
    for m in bits(shares):
        sent = shrink.astype(jnp.bfloat16)
        shrink = shrink + flip(sent, "tensor", shares, m).astype(jnp.float32)
    return finish(
        offsets,
        tile_live_rows,
        up_at.astype(jnp.int32),
        totals,
        rest,
        shrink.astype(jnp.bfloat16),
        jnp.concatenate(up_pools),
    )


def solution(mesh):
    return jax.shard_map(
        on_device,
        mesh=mesh,
        in_specs=(
            P(("groups", "dp"), "tensor"),
            P(None, None, "tensor"),
            P("dp", "tensor", None),
            P("dp", None, None, "tensor"),
            P("groups"),
            P(("groups", "dp")),
        ),
        out_specs=P(("groups", "dp"), None, "tensor"),
        check_vma=False,
    )
```

```python
import functools

import jax
import jax.numpy as jnp
from jax import lax
from jax.experimental import pallas as pl
from jax.experimental.pallas import tpu as pltpu
from jax.sharding import PartitionSpec as P


def flip(x, axis, size, mask):
    return lax.ppermute(x, axis, [(i, i ^ mask) for i in range(size)])


def bits(size, first=1):
    out = []
    while first < size:
        out.append(first)
        first *= 2
    return out


def after(value, *others):
    return lax.optimization_barrier((value,) + others)[0]


def pick_kernel(low, cuts, own_at, mate_at, mine, own, mate, own_up, mate_up, *refs):
    *downs, up, sems = refs
    moves = []
    for j in range(cuts[-1]):
        chunk = sum(j >= cut for cut in cuts[1:])
        for place, out, one, other in (
            (0, downs[chunk].at[j - cuts[chunk]], own, mate),
            (1, up.at[j], own_up, mate_up),
        ):
            sem = sems.at[2 * j + place]
            from_own = pltpu.make_async_copy(one.at[own_at[low + j]], out, sem)
            from_mate = pltpu.make_async_copy(other.at[mate_at[low + j]], out, sem)
            pl.when(mine[low + j] == 1)(from_own.start)
            pl.when(mine[low + j] != 1)(from_mate.start)
            moves.append(from_own)
    for move in moves:
        move.wait()


def pick_pages(lists, low, cuts, own, mate, own_up, mate_up):
    counts = [last - first for first, last in zip(cuts[:-1], cuts[1:])]
    return pl.pallas_call(
        functools.partial(pick_kernel, low, cuts),
        out_shape=[jax.ShapeDtypeStruct((count,) + own.shape[1:], own.dtype) for count in counts]
        + [jax.ShapeDtypeStruct((cuts[-1],) + own_up.shape[1:], own_up.dtype)],
        grid_spec=pltpu.PrefetchScalarGridSpec(
            num_scalar_prefetch=3,
            grid=(1,),
            in_specs=[pl.BlockSpec(memory_space=pl.ANY)] * 4,
            out_specs=[pl.BlockSpec((count,) + own.shape[1:], lambda i, *s: (0, 0, 0)) for count in counts]
            + [pl.BlockSpec((cuts[-1],) + own_up.shape[1:], lambda i, *s: (0, 0, 0, 0))],
            scratch_shapes=[pltpu.SemaphoreType.DMA((2 * cuts[-1],))],
        ),
        compiler_params=pltpu.CompilerParams(vmem_limit_bytes=32 << 20),
    )(*lists, own, mate, own_up, mate_up)


def blank(*shapes):
    return pl.pallas_call(
        lambda *refs: None,
        out_shape=list(shapes),
        out_specs=[pl.BlockSpec(memory_space=pl.ANY)] * len(shapes),
    )()


def side_kernel(weight, out):
    width = weight.shape[2]
    for which in range(2):
        out[0, :, which * width : (which + 1) * width] = weight[:, which, :]


def apart_kernel(weight, keys, values):
    keys[0], values[0] = weight[:, 0, :], weight[:, 1, :]


def side_by_side(at, weight, part, low, count, split=False):
    _, two, width = weight.shape
    wide = width if split else two * width
    outs = 2 if split else 1
    kernel = apart_kernel if split else side_kernel
    return pl.pallas_call(
        lambda at, *refs: kernel(*refs),
        out_shape=[jax.ShapeDtypeStruct((count, part, wide), weight.dtype)] * outs,
        grid_spec=pltpu.PrefetchScalarGridSpec(
            num_scalar_prefetch=1,
            grid=(count,),
            in_specs=[pl.BlockSpec((part, two, width), lambda j, at: (at[low + j], 0, 0))],
            out_specs=[pl.BlockSpec((1, part, wide), lambda j, at: (j, 0, 0))] * outs,
        ),
    )(at, weight)


def pack_kernel(first, at, place, x, straight, aside, picks):
    @pl.when(pl.program_id(0) == 0)
    def _():
        row = first + lax.broadcasted_iota(jnp.int32, picks.shape, 0)
        picks[...] = jnp.where(place[...] == row, 1.0, 0.0).astype(picks.dtype)

    packed = jnp.dot(picks[...], x[...], preferred_element_type=jnp.float32).astype(x.dtype)
    straight[...] = packed
    aside[...] = packed


def pack(place, x, at, part, first, last):
    rows, features = x.shape
    count = last - first
    if part % 128:
        pick = place[None, :] == jnp.arange(first, last, dtype=jnp.int32)[:, None]
        packed = jnp.dot(pick.astype(x.dtype), x, preferred_element_type=jnp.float32).astype(x.dtype)
        return packed, packed.reshape(count, -1, part)[:, at].reshape(count, features)
    return pl.pallas_call(
        functools.partial(pack_kernel, first),
        out_shape=[jax.ShapeDtypeStruct((count, features), x.dtype)] * 2,
        grid_spec=pltpu.PrefetchScalarGridSpec(
            num_scalar_prefetch=1,
            grid=(features // part,),
            in_specs=[
                pl.BlockSpec((1, rows), lambda j, at: (0, 0)),
                pl.BlockSpec((rows, part), lambda j, at: (0, j)),
            ],
            out_specs=[
                pl.BlockSpec((count, part), lambda j, at: (0, j)),
                pl.BlockSpec((count, part), lambda j, at: (0, at[j])),
            ],
            scratch_shapes=[pltpu.VMEM((count, rows), x.dtype)],
        ),
        compiler_params=pltpu.CompilerParams(vmem_limit_bytes=32 << 20),
    )(at, place.reshape(1, rows), x)


def multiply_kernel(parts, adds, x, *refs):
    weights, refs = refs[:parts], refs[parts:]
    added, outs = refs[: len(adds)], refs[len(adds) :]
    width = outs[0].shape[1]
    total, low = None, 0
    for weight in weights:
        high = low + weight.shape[0]
        piece = jnp.dot(x[:, low:high], weight[...], preferred_element_type=jnp.float32)
        total, low = piece if total is None else total + piece, high
    for i, out in enumerate(outs):
        value = total[:, i * width : (i + 1) * width]
        for ref, which in zip(added, adds):
            if which == i:
                value = value + ref[...].astype(jnp.float32)
        out[...] = value.astype(out.dtype)


def multiply(x, weights, width, added, dtype):
    rows, features = x.shape
    block = rows // 4 if rows % 64 == 0 else rows
    outs = weights[0].shape[1] // width
    adds = [(i, value) for i, values in enumerate(added) for value in values]
    piece = pl.BlockSpec((block, width), lambda j: (j, 0))
    return pl.pallas_call(
        functools.partial(multiply_kernel, len(weights), [i for i, _ in adds]),
        out_shape=[jax.ShapeDtypeStruct((rows, width), dtype)] * outs,
        grid=(rows // block,),
        in_specs=[pl.BlockSpec((block, features), lambda j: (j, 0))]
        + [pl.BlockSpec(weight.shape, lambda j: (0, 0)) for weight in weights]
        + [piece] * len(adds),
        out_specs=[piece] * outs,
        compiler_params=pltpu.CompilerParams(vmem_limit_bytes=40 << 20),
    )(x, *weights, *[value for _, value in adds])


def shrink_kernel(count, tiles, kind, places, x, *refs):
    pools, (out, pages, sems) = refs[:count], refs[count:]
    tile_rows = x.shape[0] // tiles
    for t in range(tiles):
        for number, pool in enumerate(pools):
            move = pltpu.make_async_copy(pool.at[places[t]], pages.at[t], sems.at[t])
            pl.when(kind[t] == number)(move.start)
    for t in range(tiles):
        pltpu.make_async_copy(pools[0].at[0], pages.at[t], sems.at[t]).wait()
        rows = pl.ds(t * tile_rows, tile_rows)
        out[rows, :] = jnp.dot(
            x[rows, :], pages[t], preferred_element_type=jnp.float32
        ).astype(out.dtype)


def tile_shrink(kind, places, rows, pools, tiles):
    features, columns = pools[0].shape[1:]
    return pl.pallas_call(
        functools.partial(shrink_kernel, len(pools), tiles),
        out_shape=jax.ShapeDtypeStruct((rows.shape[0], columns), jnp.bfloat16),
        grid_spec=pltpu.PrefetchScalarGridSpec(
            num_scalar_prefetch=2,
            grid=(1,),
            in_specs=[pl.BlockSpec(rows.shape, lambda i, *s: (0, 0))]
            + [pl.BlockSpec(memory_space=pl.ANY)] * len(pools),
            out_specs=pl.BlockSpec((rows.shape[0], columns), lambda i, *s: (0, 0)),
            scratch_shapes=[
                pltpu.VMEM((tiles, features, columns), pools[0].dtype),
                pltpu.SemaphoreType.DMA((tiles,)),
            ],
        ),
        compiler_params=pltpu.CompilerParams(vmem_limit_bytes=32 << 20),
    )(kind, places, rows, *pools)


def finish_kernel(count, terms, offsets, live, kind, places, *refs):
    keys, values, more_keys, more_values = refs[:4]
    parts, pools = refs[4 : 4 + terms], refs[4 + terms : 4 + terms + count]
    out, held, ups, sems = refs[4 + terms + count :]
    t = pl.program_id(0)
    tiles = ups.shape[0]
    tile_rows, two, width = out.shape
    half = ups.shape[2]
    room, rest = keys.shape[0], more_keys.shape[0]

    @pl.when(t == 0)
    def _():
        for tile in range(tiles):
            for number, pool in enumerate(pools):
                move = pltpu.make_async_copy(pool.at[places[tile]], ups.at[tile], sems.at[tile])
                pl.when(kind[tile] == number)(move.start)
        for which, (first, second) in enumerate(((keys, more_keys), (values, more_values))):
            held[which, :room] = first[...]
            held[which, room : room + rest] = second[...]
            held[which, room + rest :] = jnp.zeros((tile_rows, width), jnp.float32)

    pltpu.make_async_copy(pools[0].at[0], ups.at[t], sems.at[t]).wait()
    low = pl.multiple_of((offsets[t] // 8) * 8, 8)
    shift = offsets[t] % 8
    alive = lax.broadcasted_iota(jnp.int32, (tile_rows, width), 0) < live[t]
    shrink = parts[0][...].astype(jnp.float32)
    for part in parts[1:]:
        shrink = shrink + part[...].astype(jnp.float32)
    shrink = shrink.astype(jnp.bfloat16)
    for which in range(2):
        expand = jnp.dot(
            shrink[:, which * half : (which + 1) * half],
            ups[t, which],
            preferred_element_type=jnp.float32,
        )
        wide = held[which, pl.ds(low, tile_rows + 8), :]
        base = pltpu.roll(wide, tile_rows + 8 - shift, 0)[:tile_rows]
        out[:, which, :] = jnp.where(alive, base + expand, 0.0).astype(out.dtype)


def finish(offsets, live, kind, places, totals, rest, parts, pools):
    tiles = offsets.shape[0]
    rows, columns = parts[0].shape
    tile_rows = rows // tiles
    width = totals[0].shape[1]

    def whole(array):
        return pl.BlockSpec(array.shape, lambda t, *s: (0, 0))

    return pl.pallas_call(
        functools.partial(finish_kernel, len(pools), len(parts)),
        out_shape=jax.ShapeDtypeStruct((rows, 2, width), jnp.bfloat16),
        grid_spec=pltpu.PrefetchScalarGridSpec(
            num_scalar_prefetch=4,
            grid=(tiles,),
            in_specs=[whole(array) for array in (*totals, *rest)]
            + [pl.BlockSpec((tile_rows, columns), lambda t, *s: (t, 0))] * len(parts)
            + [pl.BlockSpec(memory_space=pl.ANY)] * len(pools),
            out_specs=pl.BlockSpec((tile_rows, 2, width), lambda t, *s: (t, 0, 0)),
            scratch_shapes=[
                pltpu.VMEM((2, rows + tile_rows, width), jnp.float32),
                pltpu.VMEM((tiles,) + pools[0].shape[1:], pools[0].dtype),
                pltpu.SemaphoreType.DMA((tiles,)),
            ],
        ),
        compiler_params=pltpu.CompilerParams(vmem_limit_bytes=48 << 20),
    )(offsets, live, kind, places, *totals, *rest, *parts, *pools)


def on_device(
    input_rows,
    key_value_weight,
    adapter_down_weight,
    adapter_up_weight,
    tile_page_index,
    tile_live_rows,
):
    groups = lax.axis_size("groups")
    ranks = lax.axis_size("dp")
    shares = lax.axis_size("tensor")
    group = lax.axis_index("groups")
    rank = lax.axis_index("dp")
    share = lax.axis_index("tensor")
    chips = ranks // 2
    chip, core = rank // 2, rank % 2
    tiles = tile_live_rows.shape[0]
    local_pages = adapter_down_weight.shape[0]
    chip_pages = 2 * local_pages
    capacity = max(2, (2 * tiles + ranks - 1) // ranks)
    most_slots = 2 * capacity
    rows, features = input_rows.shape
    tile_rows = rows // tiles
    column_width = key_value_weight.shape[2]
    half = adapter_down_weight.shape[2] // 2

    columns = 2 * column_width
    plane = groups * ranks
    part = features // plane

    line = []

    def ready(value):
        return after(value, line[-1]) if line else value

    def mark(value):
        line.append(jax.tree.leaves(value)[0])
        return value

    def wait(value):
        return mark(ready(value))

    mate_up = flip(adapter_up_weight, "dp", ranks, 1)
    mate_down = flip(adapter_down_weight, "dp", ranks, 1)

    steps = [("dp", ranks, m, (rank // m) % 2) for m in bits(ranks, 2)]
    steps += [("groups", groups, m, (group // m) % 2) for m in bits(groups)]
    steps += [("dp", ranks, 1, core)]
    over_chips = len(bits(ranks, 2))
    last_step = len(steps) - 1
    spot = sum(bit << i for i, (_, _, _, bit) in enumerate(steps))
    turns = list(range(shares - 1, 0, -1))
    order = spot ^ jnp.arange(plane, dtype=jnp.int32)
    entries = [(turns[0], 0)] + [(k, i) for k in turns[1:] for i in range(chips)]
    starts = (share ^ jnp.array([k for k, _ in entries], jnp.int32)) * plane + (
        spot ^ jnp.array([i for _, i in entries], jnp.int32)
    )
    pieces = mark(side_by_side(starts, key_value_weight, part, 0, 1, split=True))
    weights = {}
    for which in range(2):
        weights[turns[0], which] = flip(pieces[which][0], "tensor", shares, turns[0])
    first_keys = list(weights)
    for k in turns[1:]:
        piece = mark(
            side_by_side(starts, ready(key_value_weight), part, entries.index((k, 0)), chips)
        )[0]
        weights[k, 2] = flip(piece.reshape(chips * part, columns), "tensor", shares, k)
    later_keys = list(weights)[2:]
    moving = {}

    def begin(key, step):
        axis, size, m, _ = steps[step]
        moving[key, step] = flip(weights[key], axis, size, m)

    def end(key, step):
        got = wait(moving.pop((key, step)))
        weights[key] = mark(jnp.concatenate([weights[key], got]))

    def begin_last(key):
        begin(key, last_step - 1)
        begin(key, last_step)

    def go_on(key):
        got = wait(moving.pop((key, last_step - 1)))
        axis, size, m, _ = steps[last_step]
        gathered[key] = [weights[key], got, moving.pop((key, last_step)), flip(got, axis, size, m)]

    def get_all(key):
        gathered[key] = gathered[key][:2] + [wait(value) for value in gathered[key][2:]]
        return gathered[key]

    gathered = {}
    arrived = {}

    def lowest(k):
        return k & -k if k else shares

    def take(k, which, arrived):
        return [arrived.pop((k + m, which)) for m in bits(lowest(k))]

    table = tile_page_index.reshape(chips, 2 * tiles)
    page_range = jnp.arange(ranks * local_pages, dtype=jnp.int32)
    need = jnp.any(table[:, :, None] == page_range[None, None, :], axis=1)
    need = need.reshape(chips, chips, chip_pages)
    position = jnp.cumsum(need.astype(jnp.int32), axis=2) - 1
    usual = -(-5 * most_slots // 8)
    more = -(-6 * most_slots // 8)
    cuts = [0, max(1, usual // 5), max(2, 3 * usual // 5), usual]
    firsts = [0, 2 * usual, 2 * more, 2 * most_slots]
    most_pages = jnp.max(
        jnp.where(jnp.eye(chips, dtype=jnp.bool_), 0, position[:, :, -1] + 1)
    )
    slot_range = jnp.arange(2 * most_slots, dtype=jnp.int32)
    chip_range = jnp.arange(chip_pages, dtype=jnp.int32)

    offsets = jnp.cumsum(tile_live_rows) - tile_live_rows
    live_total = jnp.sum(tile_live_rows)
    live = jnp.arange(tile_rows, dtype=jnp.int32)[None, :] < tile_live_rows[:, None]
    packed_place = offsets[:, None] + jnp.arange(tile_rows, dtype=jnp.int32)[None, :]
    packed_place = jnp.where(live, packed_place, -1).reshape(rows)
    room = -(-13 * rows // 256) * 16

    listed = []
    for offset in range(1, chips):
        wanted = need[chip ^ offset, chip]
        place = position[chip ^ offset, chip]
        listed.append(
            jnp.sum(
                jnp.where(
                    wanted[None, :] & (place[None, :] == slot_range[:, None]), chip_range[None, :], 0
                ),
                axis=1,
            )
        )
    sent_lists = []
    for offset in range(1, chips):
        halves = [
            listed[offset - 1][low:high].reshape(2, (high - low) // 2)
            for low, high in zip(firsts[:-1], firsts[1:])
        ]
        halves = jnp.concatenate(halves, axis=1)
        sent = jnp.where(core == 0, halves[0], halves[1])
        mine = ((sent // local_pages) == core).astype(jnp.int32)
        at = sent % local_pages
        sent_lists.append((at * mine, at * (1 - mine), mine))

    for key in first_keys:
        weights[key] = wait(weights[key])
        begin(key, 0) if over_chips else begin_last(key)
    mate_up, mate_down = wait(mate_up), wait(mate_down)
    pools = [adapter_down_weight, mate_down]
    pool_of = {}
    crossing = {}
    picked = [
        mark(
            pick_pages(
                lists, 0, cuts, adapter_down_weight, ready(mate_down), adapter_up_weight, mate_up
            )
        )
        for lists in sent_lists
    ]
    near_ups = [flip(up, "dp", ranks, 2 * (i + 1)) for i, (*_, up) in enumerate(picked)]

    def cross(i):
        for offset in range(1, chips):
            crossing[offset, i] = flip(ready(picked[offset - 1][i]), "dp", ranks, 2 * offset)

    def share_pages(i):
        for offset in range(1, chips):
            got = wait(crossing[offset, i])
            pool_of[offset, i] = len(pools)
            pools.extend([got, flip(got, "dp", ranks, 1)])

    cross(0)
    for step in range(over_chips):
        for key in first_keys:
            end(key, step)
            begin(key, step + 1) if step + 1 < over_chips else begin_last(key)
    packed, aside = pack(packed_place, ready(input_rows), order, part, 0, room)
    mark(aside)
    near_up = jnp.concatenate([wait(up) for up in near_ups])
    up_pools = [adapter_up_weight, mate_up, near_up, flip(near_up, "dp", ranks, 1)]
    cross(1)
    for key in first_keys:
        go_on(key)
    for key in later_keys[:1]:
        weights[key] = wait(weights[key])
        begin_last(key)

    for key in first_keys:
        (sent,) = multiply(ready(aside), get_all(key), column_width, [[]], jnp.bfloat16)
        arrived[key] = flip(mark(sent), "tensor", shares, lowest(key[0]))
    share_pages(0)
    cross(2)
    at = share * plane + jnp.arange(plane, dtype=jnp.int32)
    for i, key in enumerate(later_keys):
        go_on(key)
        if i + 1 < len(later_keys):
            following = later_keys[i + 1]
            weights[following] = wait(weights[following])
            begin_last(following)
        held = get_all(key)
        if i == 0:
            own = mark(side_by_side(at, ready(key_value_weight), part, 0, plane)[0])
            own = own.reshape(features, columns)
        added = [[wait(value) for value in take(key[0], which, arrived)] for which in range(2)]
        sent = mark(multiply(ready(aside), held, column_width, added, jnp.bfloat16))
        for which in range(2):
            arrived[key[0], which] = flip(sent[which], "tensor", shares, lowest(key[0]))
        if i + 2 == len(later_keys):
            share_pages(1)
    added = [[wait(value) for value in take(0, which, arrived)] for which in range(2)]
    totals = mark(multiply(ready(packed), [own], column_width, added, jnp.float32))
    share_pages(2)

    def project_rest(operands):
        x, gathered, own = operands
        packed, aside = pack(packed_place, x, order, part, room, rows)
        arrived = {}
        for key in first_keys + later_keys:
            halves = [key[1]] if key in first_keys else [0, 1]
            added = [take(key[0], which, arrived) for which in halves]
            sent = multiply(aside, gathered[key], column_width, added, jnp.bfloat16)
            for which, value in zip(halves, sent):
                arrived[key[0], which] = flip(value, "tensor", shares, lowest(key[0]))
        added = [take(0, which, arrived) for which in range(2)]
        return multiply(packed, [own], column_width, added, jnp.float32)

    rest_shape = jax.ShapeDtypeStruct((rows - room, column_width), jnp.float32)
    rest = lax.cond(
        live_total > room,
        project_rest,
        lambda operands: blank(rest_shape, rest_shape),
        (input_rows, gathered, own),
    )

    for stage in (1, 2):

        def send_more(sources):
            low, count = firsts[stage] // 2, (firsts[stage + 1] - firsts[stage]) // 2
            got = []
            for offset in range(1, chips):
                down, up = pick_pages(sent_lists[offset - 1], low, [0, count], *sources)
                got.append((flip(down, "dp", ranks, 2 * offset), flip(up, "dp", ranks, 2 * offset)))
            down = jnp.concatenate([pair[0] for pair in got])
            up = jnp.concatenate([pair[1] for pair in got])
            return down, flip(down, "dp", ranks, 1), up, flip(up, "dp", ranks, 1)

        def send_none(sources):
            own_down, _, own_up, _ = sources
            count = (chips - 1) * (firsts[stage + 1] - firsts[stage]) // 2
            down = jax.ShapeDtypeStruct((count,) + own_down.shape[1:], own_down.dtype)
            up = jax.ShapeDtypeStruct((count,) + own_up.shape[1:], own_up.dtype)
            return tuple(blank(down, down, up, up))

        if firsts[stage + 1] > firsts[stage]:
            near, far, near_up, far_up = lax.cond(
                most_pages > firsts[stage],
                send_more,
                send_none,
                (adapter_down_weight, mate_down, adapter_up_weight, mate_up),
            )
            pool_of[stage] = len(pools)
            pools += [near, far]
            up_pools += [near_up, far_up]

    pages = tile_page_index.reshape(ranks, tiles)[rank]
    owner = pages // local_pages
    owner_chip = owner // 2
    step = owner_chip ^ chip
    entry = position[chip, owner_chip, pages % chip_pages]
    kind = jnp.where(owner == rank, 0, 1)
    places = pages % local_pages
    up_kind, up_places = kind, places
    for stage in range(3):
        count = (firsts[stage + 1] - firsts[stage]) // 2
        if count == 0:
            continue
        here = (owner_chip != chip) & (entry >= firsts[stage])
        sender, at = (entry - firsts[stage]) // count, (entry - firsts[stage]) % count
        far = (sender != core).astype(jnp.int32)
        up_kind = jnp.where(here, 2 + 2 * stage + far, up_kind)
        up_places = jnp.where(here, (step - 1) * count + at, up_places)
        if stage:
            kind = jnp.where(here, pool_of[stage] + far, kind)
            places = jnp.where(here, (step - 1) * count + at, places)
            continue
        for offset in range(1, chips):
            for i in range(3):
                chosen = here & (step == offset) & (at >= cuts[i])
                kind = jnp.where(chosen, pool_of[offset, i] + far, kind)
                places = jnp.where(chosen, at - cuts[i], places)

    shrink = tile_shrink(
        kind.astype(jnp.int32), places.astype(jnp.int32), input_rows, pools, tiles
    )
    parts = [shrink]
    for m in bits(shares):
        sent = sum(value.astype(jnp.float32) for value in parts).astype(jnp.bfloat16)
        parts.append(flip(sent, "tensor", shares, m))
    return finish(
        offsets,
        tile_live_rows,
        up_kind.astype(jnp.int32),
        up_places.astype(jnp.int32),
        totals,
        rest,
        parts,
        up_pools,
    )


def solution(mesh):
    return jax.shard_map(
        on_device,
        mesh=mesh,
        in_specs=(
            P(("groups", "dp"), "tensor"),
            P(None, None, "tensor"),
            P("dp", "tensor", None),
            P("dp", None, None, "tensor"),
            P("groups"),
            P(("groups", "dp")),
        ),
        out_specs=P(("groups", "dp"), None, "tensor"),
        check_vma=False,
    )
```

```python
import functools

import jax
import jax.numpy as jnp
from jax import lax
from jax.experimental import pallas as pl
from jax.experimental.pallas import tpu as pltpu
from jax.sharding import PartitionSpec as P


def flip(x, axis, size, mask):
    return lax.ppermute(x, axis, [(i, i ^ mask) for i in range(size)])


def bits(size, first=1):
    out = []
    while first < size:
        out.append(first)
        first *= 2
    return out


def after(value, *others):
    return lax.optimization_barrier((value,) + others)[0]


def pick_kernel(low, cuts, own_at, mate_at, mine, own, mate, own_up, mate_up, *refs):
    *downs, up, sems = refs
    moves = []
    for j in range(cuts[-1]):
        chunk = sum(j >= cut for cut in cuts[1:])
        for place, out, one, other in (
            (0, downs[chunk].at[j - cuts[chunk]], own, mate),
            (1, up.at[j], own_up, mate_up),
        ):
            sem = sems.at[2 * j + place]
            from_own = pltpu.make_async_copy(one.at[own_at[low + j]], out, sem)
            from_mate = pltpu.make_async_copy(other.at[mate_at[low + j]], out, sem)
            pl.when(mine[low + j] == 1)(from_own.start)
            pl.when(mine[low + j] != 1)(from_mate.start)
            moves.append(from_own)
    for move in moves:
        move.wait()


def pick_pages(lists, low, cuts, own, mate, own_up, mate_up):
    counts = [last - first for first, last in zip(cuts[:-1], cuts[1:])]
    return pl.pallas_call(
        functools.partial(pick_kernel, low, cuts),
        out_shape=[jax.ShapeDtypeStruct((count,) + own.shape[1:], own.dtype) for count in counts]
        + [jax.ShapeDtypeStruct((cuts[-1],) + own_up.shape[1:], own_up.dtype)],
        grid_spec=pltpu.PrefetchScalarGridSpec(
            num_scalar_prefetch=3,
            grid=(1,),
            in_specs=[pl.BlockSpec(memory_space=pl.ANY)] * 4,
            out_specs=[pl.BlockSpec((count,) + own.shape[1:], lambda i, *s: (0, 0, 0)) for count in counts]
            + [pl.BlockSpec((cuts[-1],) + own_up.shape[1:], lambda i, *s: (0, 0, 0, 0))],
            scratch_shapes=[pltpu.SemaphoreType.DMA((2 * cuts[-1],))],
        ),
        compiler_params=pltpu.CompilerParams(vmem_limit_bytes=32 << 20),
    )(*lists, own, mate, own_up, mate_up)


def blank(*shapes):
    return pl.pallas_call(
        lambda *refs: None,
        out_shape=list(shapes),
        out_specs=[pl.BlockSpec(memory_space=pl.ANY)] * len(shapes),
    )()


def side_kernel(weight, out):
    width = weight.shape[2]
    for which in range(2):
        out[0, :, which * width : (which + 1) * width] = weight[:, which, :]


def apart_kernel(weight, keys, values):
    keys[0], values[0] = weight[:, 0, :], weight[:, 1, :]


def side_by_side(at, weight, part, low, count, split=False):
    _, two, width = weight.shape
    wide = width if split else two * width
    outs = 2 if split else 1
    kernel = apart_kernel if split else side_kernel
    return pl.pallas_call(
        lambda at, *refs: kernel(*refs),
        out_shape=[jax.ShapeDtypeStruct((count, part, wide), weight.dtype)] * outs,
        grid_spec=pltpu.PrefetchScalarGridSpec(
            num_scalar_prefetch=1,
            grid=(count,),
            in_specs=[pl.BlockSpec((part, two, width), lambda j, at: (at[low + j], 0, 0))],
            out_specs=[pl.BlockSpec((1, part, wide), lambda j, at: (j, 0, 0))] * outs,
        ),
    )(at, weight)


def pack_kernel(first, at, place, x, straight, aside, picks):
    @pl.when(pl.program_id(0) == 0)
    def _():
        row = first + lax.broadcasted_iota(jnp.int32, picks.shape, 0)
        picks[...] = jnp.where(place[...] == row, 1.0, 0.0).astype(picks.dtype)

    packed = jnp.dot(picks[...], x[...], preferred_element_type=jnp.float32).astype(x.dtype)
    straight[...] = packed
    aside[...] = packed


def pack(place, x, at, part, first, last):
    rows, features = x.shape
    count = last - first
    if part % 128:
        pick = place[None, :] == jnp.arange(first, last, dtype=jnp.int32)[:, None]
        packed = jnp.dot(pick.astype(x.dtype), x, preferred_element_type=jnp.float32).astype(x.dtype)
        return packed, packed.reshape(count, -1, part)[:, at].reshape(count, features)
    return pl.pallas_call(
        functools.partial(pack_kernel, first),
        out_shape=[jax.ShapeDtypeStruct((count, features), x.dtype)] * 2,
        grid_spec=pltpu.PrefetchScalarGridSpec(
            num_scalar_prefetch=1,
            grid=(features // part,),
            in_specs=[
                pl.BlockSpec((1, rows), lambda j, at: (0, 0)),
                pl.BlockSpec((rows, part), lambda j, at: (0, j)),
            ],
            out_specs=[
                pl.BlockSpec((count, part), lambda j, at: (0, j)),
                pl.BlockSpec((count, part), lambda j, at: (0, at[j])),
            ],
            scratch_shapes=[pltpu.VMEM((count, rows), x.dtype)],
        ),
        compiler_params=pltpu.CompilerParams(vmem_limit_bytes=32 << 20),
    )(at, place.reshape(1, rows), x)


def multiply_kernel(parts, x, *refs):
    weights, added, out = refs[:parts], refs[parts:-1], refs[-1]
    total, low = None, 0
    for weight in weights:
        high = low + weight.shape[0]
        piece = jnp.dot(x[:, low:high], weight[...], preferred_element_type=jnp.float32)
        total, low = piece if total is None else total + piece, high
    for ref in added:
        total = total + ref[...].astype(jnp.float32)
    out[...] = total.astype(out.dtype)


def multiply(x, weights, added, dtype):
    rows, features = x.shape
    block = rows // 4 if rows % 64 == 0 else rows
    width = weights[0].shape[1]
    piece = pl.BlockSpec((block, width), lambda j: (j, 0))
    return pl.pallas_call(
        functools.partial(multiply_kernel, len(weights)),
        out_shape=jax.ShapeDtypeStruct((rows, width), dtype),
        grid=(rows // block,),
        in_specs=[pl.BlockSpec((block, features), lambda j: (j, 0))]
        + [pl.BlockSpec(weight.shape, lambda j: (0, 0)) for weight in weights]
        + [piece] * len(added),
        out_specs=piece,
        compiler_params=pltpu.CompilerParams(vmem_limit_bytes=40 << 20),
    )(x, *weights, *added)


def shrink_kernel(count, tiles, kind, places, *refs):
    (own_x, mate_x), pools, outs = refs[:2], refs[2 : 2 + count], refs[2 + count : 4 + count]
    rows_in, pages, row_sems, sems = refs[4 + count :]
    tile_rows = outs[0].shape[0] // tiles
    for i in range(2 * tiles):
        rows = pl.ds(i % tiles * tile_rows, tile_rows)
        x = own_x if i < tiles else mate_x
        for number, pool in enumerate(pools):
            move = pltpu.make_async_copy(pool.at[places[i]], pages.at[i], sems.at[i])
            pl.when(kind[i] == number)(move.start)
        move = pltpu.make_async_copy(x.at[rows], rows_in.at[i], row_sems.at[i])
        pl.when(kind[i] >= 0)(move.start)
    for i in range(2 * tiles):
        rows = pl.ds(i % tiles * tile_rows, tile_rows)
        x, out = (own_x, outs[0]) if i < tiles else (mate_x, outs[1])

        @pl.when(kind[i] >= 0)
        def _(i=i, rows=rows, x=x, out=out):
            pltpu.make_async_copy(pools[0].at[0], pages.at[i], sems.at[i]).wait()
            pltpu.make_async_copy(x.at[rows], rows_in.at[i], row_sems.at[i]).wait()
            out[rows, :] = jnp.dot(
                rows_in[i], pages[i], preferred_element_type=jnp.float32
            ).astype(out.dtype)

        @pl.when(kind[i] < 0)
        def _(rows=rows, out=out):
            out[rows, :] = jnp.zeros((tile_rows, out.shape[1]), out.dtype)


def tile_shrink(kind, places, own_x, mate_x, pools, tiles):
    features, columns = pools[0].shape[1:]
    rows = own_x.shape[0]
    out = pl.BlockSpec((rows, columns), lambda i, *s: (0, 0))
    return pl.pallas_call(
        functools.partial(shrink_kernel, len(pools), tiles),
        out_shape=[jax.ShapeDtypeStruct((rows, columns), jnp.bfloat16)] * 2,
        grid_spec=pltpu.PrefetchScalarGridSpec(
            num_scalar_prefetch=2,
            grid=(1,),
            in_specs=[pl.BlockSpec(memory_space=pl.ANY)] * (2 + len(pools)),
            out_specs=[out, out],
            scratch_shapes=[
                pltpu.VMEM((2 * tiles, rows // tiles, features), own_x.dtype),
                pltpu.VMEM((2 * tiles, features, columns), pools[0].dtype),
                pltpu.SemaphoreType.DMA((2 * tiles,)),
                pltpu.SemaphoreType.DMA((2 * tiles,)),
            ],
        ),
        compiler_params=pltpu.CompilerParams(vmem_limit_bytes=48 << 20),
    )(kind, places, own_x, mate_x, *pools)


def finish_kernel(count, terms, offsets, live, kind, places, *refs):
    base, more = refs[:2]
    parts, pools = refs[2 : 2 + terms], refs[2 + terms : 2 + terms + count]
    out, held, ups, sems = refs[2 + terms + count :]
    t = pl.program_id(0)
    tiles = ups.shape[0]
    tile_rows, two, width = out.shape
    half = ups.shape[2]
    room, rest = base.shape[0], more.shape[0]

    @pl.when(t == 0)
    def _():
        for tile in range(tiles):
            for number, pool in enumerate(pools):
                move = pltpu.make_async_copy(pool.at[places[tile]], ups.at[tile], sems.at[tile])
                pl.when(kind[tile] == number)(move.start)
        held[:room] = base[...]
        held[room : room + rest] = more[...]
        held[room + rest :] = jnp.zeros((tile_rows, 2 * width), jnp.float32)

    pltpu.make_async_copy(pools[0].at[0], ups.at[t], sems.at[t]).wait()
    low = pl.multiple_of((offsets[t] // 8) * 8, 8)
    shift = offsets[t] % 8
    alive = lax.broadcasted_iota(jnp.int32, (tile_rows, width), 0) < live[t]
    shrink = parts[0][...].astype(jnp.float32)
    for part in parts[1:]:
        shrink = shrink + part[...].astype(jnp.float32)
    shrink = shrink.astype(jnp.bfloat16)
    for which in range(2):
        expand = jnp.dot(
            shrink[:, which * half : (which + 1) * half],
            ups[t, which],
            preferred_element_type=jnp.float32,
        )
        wide = held[pl.ds(low, tile_rows + 8), which * width : (which + 1) * width]
        part = pltpu.roll(wide, tile_rows + 8 - shift, 0)[:tile_rows]
        out[:, which, :] = jnp.where(alive, part + expand, 0.0).astype(out.dtype)


def finish(offsets, live, kind, places, totals, rest, parts, pools):
    tiles = offsets.shape[0]
    rows, columns = parts[0].shape
    tile_rows = rows // tiles
    width = totals.shape[1] // 2

    def whole(array):
        return pl.BlockSpec(array.shape, lambda t, *s: (0, 0))

    return pl.pallas_call(
        functools.partial(finish_kernel, len(pools), len(parts)),
        out_shape=jax.ShapeDtypeStruct((rows, 2, width), jnp.bfloat16),
        grid_spec=pltpu.PrefetchScalarGridSpec(
            num_scalar_prefetch=4,
            grid=(tiles,),
            in_specs=[whole(totals), whole(rest)]
            + [pl.BlockSpec((tile_rows, columns), lambda t, *s: (t, 0))] * len(parts)
            + [pl.BlockSpec(memory_space=pl.ANY)] * len(pools),
            out_specs=pl.BlockSpec((tile_rows, 2, width), lambda t, *s: (t, 0, 0)),
            scratch_shapes=[
                pltpu.VMEM((rows + tile_rows, 2 * width), jnp.float32),
                pltpu.VMEM((tiles,) + pools[0].shape[1:], pools[0].dtype),
                pltpu.SemaphoreType.DMA((tiles,)),
            ],
        ),
        compiler_params=pltpu.CompilerParams(vmem_limit_bytes=48 << 20),
    )(offsets, live, kind, places, totals, rest, *parts, *pools)


def on_device(
    input_rows,
    key_value_weight,
    adapter_down_weight,
    adapter_up_weight,
    tile_page_index,
    tile_live_rows,
):
    groups = lax.axis_size("groups")
    ranks = lax.axis_size("dp")
    shares = lax.axis_size("tensor")
    group = lax.axis_index("groups")
    rank = lax.axis_index("dp")
    share = lax.axis_index("tensor")
    chips = ranks // 2
    chip, core = rank // 2, rank % 2
    tiles = tile_live_rows.shape[0]
    local_pages = adapter_down_weight.shape[0]
    chip_pages = 2 * local_pages
    capacity = max(2, (2 * tiles + ranks - 1) // ranks)
    most_slots = 2 * capacity
    rows, features = input_rows.shape
    tile_rows = rows // tiles
    column_width = key_value_weight.shape[2]
    half = adapter_down_weight.shape[2] // 2

    columns = 2 * column_width
    plane = groups * ranks
    part = features // plane

    line = []

    def ready(value):
        return after(value, line[-1]) if line else value

    def mark(value):
        line.append(jax.tree.leaves(value)[0])
        return value

    def wait(value):
        return mark(ready(value))

    mate_up = flip(adapter_up_weight, "dp", ranks, 1)
    mate_down = flip(adapter_down_weight, "dp", ranks, 1)
    mate_rows = flip(input_rows, "dp", ranks, 1)

    steps = [("dp", ranks, m, (rank // m) % 2) for m in bits(ranks, 2)]
    steps += [("groups", groups, m, (group // m) % 2) for m in bits(groups)]
    steps += [("dp", ranks, 1, core)]
    over_chips = len(bits(ranks, 2))
    last_step = len(steps) - 1
    spot = sum(bit << i for i, (_, _, _, bit) in enumerate(steps))
    turns = list(range(shares - 1, 0, -1))
    order = spot ^ jnp.arange(plane, dtype=jnp.int32)
    entries = [(turns[0], 0)] + [(k, i) for k in turns[1:] for i in range(chips)]
    starts = (share ^ jnp.array([k for k, _ in entries], jnp.int32)) * plane + (
        spot ^ jnp.array([i for _, i in entries], jnp.int32)
    )
    weights = {}
    for k in turns:
        count = 1 if k == turns[0] else chips
        piece = mark(
            side_by_side(starts, ready(key_value_weight), part, entries.index((k, 0)), count)
        )[0]
        weights[k] = piece.reshape(count * part, columns)
        if k == turns[0]:
            weights[k] = flip(weights[k], "tensor", shares, k)

    moving = {}

    def begin(key, step):
        axis, size, m, _ = steps[step]
        moving[key, step] = flip(weights[key], axis, size, m)

    def end(key, step):
        got = wait(moving.pop((key, step)))
        weights[key] = mark(jnp.concatenate([weights[key], got]))

    def go_on(key):
        got = wait(moving.pop((key, last_step - 1)))
        axis, size, m, _ = steps[last_step]
        gathered[key] = [weights[key], got] + [flip(v, axis, size, m) for v in (weights[key], got)]

    def get_all(key):
        gathered[key] = gathered[key][:2] + [wait(value) for value in gathered[key][2:]]
        return gathered[key]

    gathered = {}
    arrived = {}

    def lowest(k):
        return k & -k if k else shares

    def take(k, arrived):
        return [arrived.pop(k + m) for m in bits(lowest(k))]

    table = tile_page_index.reshape(chips, 2 * tiles)
    page_range = jnp.arange(ranks * local_pages, dtype=jnp.int32)
    need = jnp.any(table[:, :, None] == page_range[None, None, :], axis=1)
    need = need.reshape(chips, chips, chip_pages)
    position = jnp.cumsum(need.astype(jnp.int32), axis=2) - 1
    usual = -(-5 * most_slots // 8)
    more = -(-6 * most_slots // 8)
    cuts = [0, max(1, 2 * usual // 5), max(2, 4 * usual // 5), usual]
    firsts = [0, 2 * usual, 2 * more, 2 * most_slots]
    most_pages = jnp.max(
        jnp.where(jnp.eye(chips, dtype=jnp.bool_), 0, position[:, :, -1] + 1)
    )
    slot_range = jnp.arange(2 * most_slots, dtype=jnp.int32)
    chip_range = jnp.arange(chip_pages, dtype=jnp.int32)

    offsets = jnp.cumsum(tile_live_rows) - tile_live_rows
    live_total = jnp.sum(tile_live_rows)
    live = jnp.arange(tile_rows, dtype=jnp.int32)[None, :] < tile_live_rows[:, None]
    packed_place = offsets[:, None] + jnp.arange(tile_rows, dtype=jnp.int32)[None, :]
    packed_place = jnp.where(live, packed_place, -1).reshape(rows)
    room = -(-13 * rows // 256) * 16

    listed = []
    for offset in range(1, chips):
        wanted = need[chip ^ offset, chip]
        place = position[chip ^ offset, chip]
        listed.append(
            jnp.sum(
                jnp.where(
                    wanted[None, :] & (place[None, :] == slot_range[:, None]), chip_range[None, :], 0
                ),
                axis=1,
            )
        )
    sent_lists = []
    for offset in range(1, chips):
        halves = [
            listed[offset - 1][low:high].reshape(2, (high - low) // 2)
            for low, high in zip(firsts[:-1], firsts[1:])
        ]
        halves = jnp.concatenate(halves, axis=1)
        sent = jnp.where(core == 0, halves[0], halves[1])
        mine = ((sent // local_pages) == core).astype(jnp.int32)
        at = sent % local_pages
        sent_lists.append((at * mine, at * (1 - mine), mine))

    def locate(pages):
        owner = pages // local_pages
        entry = position[chip, owner // 2, pages % chip_pages]
        return pages % local_pages, owner, (owner // 2) ^ chip, entry

    page_lists = tile_page_index.reshape(ranks, tiles)
    at_home, owner, step, entry = locate(
        jnp.concatenate([page_lists[rank], page_lists[rank ^ 1]])
    )
    kind, places = jnp.where(owner == rank, 0, -1), at_home
    up_kind, up_places = jnp.where(owner == rank, 0, 1), at_home
    for stage in range(3):
        count = (firsts[stage + 1] - firsts[stage]) // 2
        if count == 0:
            continue
        here = (step != 0) & (entry >= firsts[stage])
        sender, at = (entry - firsts[stage]) // count, (entry - firsts[stage]) % count
        far = (sender != core).astype(jnp.int32)
        up_kind = jnp.where(here, 2 + 2 * stage + far, up_kind)
        up_places = jnp.where(here, (step - 1) * count + at, up_places)
        if stage:
            kind = jnp.where(here, (len(cuts) - 1) * (chips - 1) + stage, kind)
            places = jnp.where(here, (step - 1) * count + at, places)
        else:
            for offset in range(1, chips):
                for i in range(len(cuts) - 1):
                    chosen = here & (step == offset) & (at >= cuts[i])
                    kind = jnp.where(chosen, i * (chips - 1) + offset, kind)
                    places = jnp.where(chosen, at - cuts[i], places)
        kind = jnp.where(here & (far == 1), -1, kind)
    up_kind = up_kind[:tiles].astype(jnp.int32)
    up_places = up_places[:tiles].astype(jnp.int32)
    kind, places = kind.astype(jnp.int32), places.astype(jnp.int32)

    mate_up = wait(mate_up)
    first = turns[0]
    weights[first] = wait(weights[first])
    begin(first, 0)
    for k in turns[1:]:
        weights[k] = flip(ready(weights[k]), "tensor", shares, k)
    mate_down, mate_rows = wait(mate_down), wait(mate_rows)
    pools = [adapter_down_weight]
    crossing = {}
    picked = [
        mark(
            pick_pages(
                lists, 0, cuts, adapter_down_weight, ready(mate_down), adapter_up_weight, mate_up
            )
        )
        for lists in sent_lists
    ]

    def cross(i):
        for offset in range(1, chips):
            crossing[offset, i] = flip(ready(picked[offset - 1][i]), "dp", ranks, 2 * offset)

    def share_pages(i):
        for offset in range(1, chips):
            pools.append(wait(crossing[offset, i]))

    cross(0)
    for value in (kind, places, up_kind, up_places):
        mark(value)
    for step in range(over_chips):
        end(first, step)
        begin(first, step + 1)
    packed, aside = pack(packed_place, ready(input_rows), order, part, 0, room)
    mark(aside)
    for k in turns[1:]:
        weights[k] = wait(weights[k])
        begin(k, last_step - 1)
    go_on(first)

    def product(k):
        added = [wait(value) for value in take(k, arrived)]
        sent = mark(multiply(ready(aside), gathered[k], added, jnp.bfloat16))
        arrived[k] = flip(sent, "tensor", shares, lowest(k))

    get_all(first)
    product(first)
    share_pages(0)
    cross(1)
    at = share * plane + jnp.arange(plane, dtype=jnp.int32)
    own = mark(side_by_side(at, ready(key_value_weight), part, 0, plane)[0])
    own = own.reshape(features, columns)
    near_ups = [
        flip(ready(up), "dp", ranks, 2 * (i + 1)) for i, (*_, up) in enumerate(picked)
    ]
    cross(2)
    for k in turns[1:]:
        go_on(k)
    for k in turns[1:]:
        get_all(k)
        product(k)
    share_pages(1)
    usual_up = jnp.concatenate([wait(up) for up in near_ups])
    usual_ups = [usual_up, flip(usual_up, "dp", ranks, 1)]

    up_pools = [adapter_up_weight, mate_up]
    for stage in (1, 2):

        def send_more(sources):
            low, count = firsts[stage] // 2, (firsts[stage + 1] - firsts[stage]) // 2
            got = []
            for offset in range(1, chips):
                down, up = pick_pages(sent_lists[offset - 1], low, [0, count], *sources)
                got.append((flip(down, "dp", ranks, 2 * offset), flip(up, "dp", ranks, 2 * offset)))
            down = jnp.concatenate([pair[0] for pair in got])
            up = jnp.concatenate([pair[1] for pair in got])
            return down, up, flip(up, "dp", ranks, 1)

        def send_none(sources):
            own_down, _, own_up, _ = sources
            count = (chips - 1) * (firsts[stage + 1] - firsts[stage]) // 2
            down = jax.ShapeDtypeStruct((count,) + own_down.shape[1:], own_down.dtype)
            up = jax.ShapeDtypeStruct((count,) + own_up.shape[1:], own_up.dtype)
            return tuple(blank(down, up, up))

        if firsts[stage + 1] > firsts[stage]:
            near, near_up, far_up = lax.cond(
                most_pages > firsts[stage],
                send_more,
                send_none,
                (ready(adapter_down_weight), mate_down, adapter_up_weight, mate_up),
            )
            pools.append(near)
            up_pools += [near_up, far_up]

    more_pools = pools[1 + 2 * (chips - 1) :]
    del pools[1 + 2 * (chips - 1) :]
    share_pages(2)
    pools += more_pools

    shrink, mate_shrink = tile_shrink(
        kind,
        places,
        ready(input_rows),
        mate_rows,
        pools,
        tiles,
    )
    shrink = shrink + wait(flip(mark(mate_shrink), "dp", ranks, 1))
    parts = [mark(shrink)]
    for m in bits(shares):
        sent = sum(value.astype(jnp.float32) for value in parts).astype(jnp.bfloat16)
        parts.append(flip(sent, "tensor", shares, m))
        if m == 1:
            final = [wait(value) for value in take(0, arrived)]
            totals = mark(multiply(ready(packed), [own], final, jnp.float32))
            parts[-1] = wait(parts[-1])
            up_pools[2:2] = usual_ups
        else:
            parts[-1] = wait(parts[-1])

    def project_rest(operands):
        x, gathered, own = operands
        packed, aside = pack(packed_place, x, order, part, room, rows)
        arrived = {}
        for k in turns:
            sent = multiply(aside, gathered[k], take(k, arrived), jnp.bfloat16)
            arrived[k] = flip(sent, "tensor", shares, lowest(k))
        return multiply(packed, [own], take(0, arrived), jnp.float32)

    rest_shape = jax.ShapeDtypeStruct((rows - room, columns), jnp.float32)
    rest = lax.cond(
        live_total > room,
        project_rest,
        lambda operands: blank(rest_shape)[0],
        (input_rows, gathered, own),
    )
    return finish(
        offsets,
        tile_live_rows,
        up_kind,
        up_places,
        totals,
        rest,
        parts,
        up_pools,
    )


def solution(mesh):
    return jax.shard_map(
        on_device,
        mesh=mesh,
        in_specs=(
            P(("groups", "dp"), "tensor"),
            P(None, None, "tensor"),
            P("dp", "tensor", None),
            P("dp", None, None, "tensor"),
            P("groups"),
            P(("groups", "dp")),
        ),
        out_specs=P(("groups", "dp"), None, "tensor"),
        check_vma=False,
    )
```

```python
import functools

import jax
import jax.numpy as jnp
from jax import lax
from jax.experimental import pallas as pl
from jax.experimental.pallas import tpu as pltpu
from jax.sharding import PartitionSpec as P


def flip(x, axis, size, mask):
    return lax.ppermute(x, axis, [(i, i ^ mask) for i in range(size)])


def bits(size, first=1):
    out = []
    while first < size:
        out.append(first)
        first *= 2
    return out


def after(value, *others):
    return lax.optimization_barrier((value,) + others)[0]


def pick_kernel(low, cuts, own_at, mate_at, mine, own, mate, own_up, mate_up, *refs):
    *downs, up, sems = refs
    moves = []
    for j in range(cuts[-1]):
        chunk = sum(j >= cut for cut in cuts[1:])
        for place, out, one, other in (
            (0, downs[chunk].at[j - cuts[chunk]], own, mate),
            (1, up.at[j], own_up, mate_up),
        ):
            sem = sems.at[2 * j + place]
            from_own = pltpu.make_async_copy(one.at[own_at[low + j]], out, sem)
            from_mate = pltpu.make_async_copy(other.at[mate_at[low + j]], out, sem)
            pl.when(mine[low + j] == 1)(from_own.start)
            pl.when(mine[low + j] != 1)(from_mate.start)
            moves.append(from_own)
    for move in moves:
        move.wait()


def pick_pages(lists, low, cuts, own, mate, own_up, mate_up):
    counts = [last - first for first, last in zip(cuts[:-1], cuts[1:])]
    return pl.pallas_call(
        functools.partial(pick_kernel, low, cuts),
        out_shape=[jax.ShapeDtypeStruct((count,) + own.shape[1:], own.dtype) for count in counts]
        + [jax.ShapeDtypeStruct((cuts[-1],) + own_up.shape[1:], own_up.dtype)],
        grid_spec=pltpu.PrefetchScalarGridSpec(
            num_scalar_prefetch=3,
            grid=(1,),
            in_specs=[pl.BlockSpec(memory_space=pltpu.HBM)] * 4,
            out_specs=[pl.BlockSpec((count,) + own.shape[1:], lambda i, *s: (0, 0, 0)) for count in counts]
            + [pl.BlockSpec((cuts[-1],) + own_up.shape[1:], lambda i, *s: (0, 0, 0, 0))],
            scratch_shapes=[pltpu.SemaphoreType.DMA((2 * cuts[-1],))],
        ),
        compiler_params=pltpu.CompilerParams(vmem_limit_bytes=32 << 20),
    )(*lists, own, mate, own_up, mate_up)


def blank(*shapes):
    return pl.pallas_call(
        lambda *refs: None,
        out_shape=list(shapes),
        out_specs=[pl.BlockSpec(memory_space=pltpu.HBM)] * len(shapes),
    )()


def side_kernel(weight, out):
    out[0] = weight[...].reshape(out.shape[1:])


def side_by_side(at, weight, part, low, count):
    _, two, width = weight.shape
    return pl.pallas_call(
        lambda at, *refs: side_kernel(*refs),
        out_shape=[jax.ShapeDtypeStruct((count, part, two * width), weight.dtype)],
        grid_spec=pltpu.PrefetchScalarGridSpec(
            num_scalar_prefetch=1,
            grid=(count,),
            in_specs=[pl.BlockSpec((part, two, width), lambda j, at: (at[low + j], 0, 0))],
            out_specs=[pl.BlockSpec((1, part, two * width), lambda j, at: (j, 0, 0))],
        ),
    )(at, weight)


def pack_kernel(first, at, place, x, straight, aside, picks):
    @pl.when(pl.program_id(0) == 0)
    def _():
        row = first + lax.broadcasted_iota(jnp.int32, picks.shape, 0)
        picks[...] = jnp.where(place[...] == row, 1.0, 0.0).astype(picks.dtype)

    packed = jnp.dot(picks[...], x[...], preferred_element_type=jnp.float32).astype(x.dtype)
    straight[...] = packed
    aside[...] = packed


def pack(place, x, at, part, first, last):
    rows, features = x.shape
    count = last - first
    if part % 128:
        pick = place[None, :] == jnp.arange(first, last, dtype=jnp.int32)[:, None]
        packed = jnp.dot(pick.astype(x.dtype), x, preferred_element_type=jnp.float32).astype(x.dtype)
        return packed, packed.reshape(count, -1, part)[:, at].reshape(count, features)
    return pl.pallas_call(
        functools.partial(pack_kernel, first),
        out_shape=[jax.ShapeDtypeStruct((count, features), x.dtype)] * 2,
        grid_spec=pltpu.PrefetchScalarGridSpec(
            num_scalar_prefetch=1,
            grid=(features // part,),
            in_specs=[
                pl.BlockSpec((1, rows), lambda j, at: (0, 0)),
                pl.BlockSpec((rows, part), lambda j, at: (0, j)),
            ],
            out_specs=[
                pl.BlockSpec((count, part), lambda j, at: (0, j)),
                pl.BlockSpec((count, part), lambda j, at: (0, at[j])),
            ],
            scratch_shapes=[pltpu.VMEM((count, rows), x.dtype)],
        ),
        compiler_params=pltpu.CompilerParams(vmem_limit_bytes=32 << 20),
    )(at, place.reshape(1, rows), x)


def add_up_kernel(*refs):
    total = refs[0][...].astype(jnp.float32)
    for ref in refs[1:-1]:
        total = total + ref[...].astype(jnp.float32)
    refs[-1][...] = total.astype(refs[-1].dtype)


def add_up(values, dtype):
    rows, width = values[0].shape
    block = rows // 2 if rows % 32 == 0 else rows
    piece = pl.BlockSpec((block, width), lambda j: (j, 0))
    return pl.pallas_call(
        add_up_kernel,
        out_shape=jax.ShapeDtypeStruct((rows, width), dtype),
        grid=(rows // block,),
        in_specs=[piece] * len(values),
        out_specs=piece,
        compiler_params=pltpu.CompilerParams(vmem_limit_bytes=32 << 20),
    )(*values)


def multiply_kernel(parts, adds, x, *refs):
    weights, added, refs = refs[:parts], refs[parts : parts + adds], refs[parts + adds :]
    out = refs[0]
    j = pl.program_id(0)
    block = x.shape[0]
    moves = []
    if adds:
        added_in, sems = refs[1:]
        moves = [
            pltpu.make_async_copy(ref, added_in.at[i], sems.at[i]) for i, ref in enumerate(added)
        ]

    @pl.when(j == 0)
    def _():
        for move in moves:
            move.start()

    total, low = None, 0
    for weight in weights:
        high = low + weight.shape[0]
        piece = jnp.dot(x[:, low:high], weight[...], preferred_element_type=jnp.float32)
        total, low = piece if total is None else total + piece, high

    @pl.when(j == 0)
    def _():
        for move in moves:
            move.wait()

    for i in range(adds):
        rows = pl.ds(pl.multiple_of(j * block, block), block)
        total = total + added_in[i, rows, :].astype(jnp.float32)
    out[...] = total.astype(out.dtype)


def multiply(x, weights, added, dtype, spare=0):
    rows, features = x.shape
    block = rows // 2 if rows % 32 == 0 else rows
    width = weights[0].shape[1]
    scratch = []
    if added:
        scratch = [
            pltpu.VMEM((len(added), rows, width), added[0].dtype),
            pltpu.SemaphoreType.DMA((len(added),)),
        ]
    return pl.pallas_call(
        functools.partial(multiply_kernel, len(weights), len(added)),
        out_shape=jax.ShapeDtypeStruct((rows + spare, width), dtype),
        grid=(rows // block,),
        in_specs=[pl.BlockSpec((block, features), lambda j: (j, 0))]
        + [pl.BlockSpec(weight.shape, lambda j: (0, 0)) for weight in weights]
        + [pl.BlockSpec(memory_space=pl.ANY)] * len(added),
        out_specs=pl.BlockSpec((block, width), lambda j: (j, 0)),
        scratch_shapes=scratch,
        compiler_params=pltpu.CompilerParams(vmem_limit_bytes=40 << 20),
    )(x, *weights, *added)


def shrink_kernel(count, tiles, kind, places, *refs):
    (own_x, mate_x), pools, outs = refs[:2], refs[2 : 2 + count], refs[2 + count : 4 + count]
    rows_in, pages, row_sems, sems = refs[4 + count :]
    tile_rows = outs[0].shape[0] // tiles
    for i in range(2 * tiles):
        rows = pl.ds(i % tiles * tile_rows, tile_rows)
        x = own_x if i < tiles else mate_x
        for number, pool in enumerate(pools):
            move = pltpu.make_async_copy(pool.at[places[i]], pages.at[i], sems.at[i])
            pl.when(kind[i] == number)(move.start)
        move = pltpu.make_async_copy(x.at[rows], rows_in.at[i], row_sems.at[i])
        pl.when(kind[i] >= 0)(move.start)
    for i in range(2 * tiles):
        rows = pl.ds(i % tiles * tile_rows, tile_rows)
        x, out = (own_x, outs[0]) if i < tiles else (mate_x, outs[1])

        @pl.when(kind[i] >= 0)
        def _(i=i, rows=rows, x=x, out=out):
            pltpu.make_async_copy(pools[0].at[0], pages.at[i], sems.at[i]).wait()
            pltpu.make_async_copy(x.at[rows], rows_in.at[i], row_sems.at[i]).wait()
            out[rows, :] = jnp.dot(
                rows_in[i], pages[i], preferred_element_type=jnp.float32
            ).astype(out.dtype)

        @pl.when(kind[i] < 0)
        def _(rows=rows, out=out):
            out[rows, :] = jnp.zeros((tile_rows, out.shape[1]), out.dtype)


def tile_shrink(kind, places, own_x, mate_x, pools, tiles):
    features, columns = pools[0].shape[1:]
    rows = own_x.shape[0]
    out = pl.BlockSpec((rows, columns), lambda i, *s: (0, 0))
    return pl.pallas_call(
        functools.partial(shrink_kernel, len(pools), tiles),
        out_shape=[jax.ShapeDtypeStruct((rows, columns), jnp.bfloat16)] * 2,
        grid_spec=pltpu.PrefetchScalarGridSpec(
            num_scalar_prefetch=2,
            grid=(1,),
            in_specs=[pl.BlockSpec(memory_space=pltpu.HBM)] * (2 + len(pools)),
            out_specs=[out, out],
            scratch_shapes=[
                pltpu.VMEM((2 * tiles, rows // tiles, features), own_x.dtype),
                pltpu.VMEM((2 * tiles, features, columns), pools[0].dtype),
                pltpu.SemaphoreType.DMA((2 * tiles,)),
                pltpu.SemaphoreType.DMA((2 * tiles,)),
            ],
        ),
        compiler_params=pltpu.CompilerParams(vmem_limit_bytes=48 << 20),
    )(kind, places, own_x, mate_x, *pools)


def finish_kernel(count, terms, offsets, live, kind, places, *refs):
    base, more = refs[:2]
    parts, pools = refs[2 : 2 + terms], refs[2 + terms : 2 + terms + count]
    out, held, ups, terms_in, sems, term_sems, more_sem = refs[2 + terms + count :]
    t = pl.program_id(0)
    tiles = ups.shape[0]
    tile_rows, width = parts[0].shape[0] // tiles, out.shape[2]
    per_step = out.shape[0] // tile_rows
    half = ups.shape[2]
    rest = more.shape[0]
    rows = held.shape[0] - tile_rows
    room = rows - rest
    over = offsets[tiles - 1] + live[tiles - 1] > room

    part_moves = [
        pltpu.make_async_copy(part, terms_in.at[i], term_sems.at[i]) for i, part in enumerate(parts)
    ]

    @pl.when(t == 0)
    def _():
        for move in part_moves:
            move.start()
        for tile in range(tiles):
            for number, pool in enumerate(pools):
                move = pltpu.make_async_copy(pool.at[places[tile]], ups.at[tile], sems.at[tile])
                pl.when(kind[tile] == number)(move.start)

    @pl.when((t == 0) & over)
    def _():
        move = pltpu.make_async_copy(more, held.at[pl.ds(room, rest)], more_sem)
        move.start()
        held[:room] = base[:room]
        held[rows:] = jnp.zeros((tile_rows, 2 * width), jnp.float32)
        move.wait()

    @pl.when(t == 0)
    def _():
        for move in part_moves:
            move.wait()

    def put(tile, source, rows):
        low = pl.multiple_of((offsets[tile] // 8) * 8, 8)
        alive = lax.broadcasted_iota(jnp.int32, (tile_rows, 2 * width), 0) < live[tile]
        span = pl.ds(pl.multiple_of(tile * tile_rows, tile_rows), tile_rows)
        shrink = terms_in[0, span, :].astype(jnp.float32)
        for i in range(1, terms):
            shrink = shrink + terms_in[i, span, :].astype(jnp.float32)
        shrink = shrink.astype(jnp.bfloat16)
        wide = source[pl.ds(low, tile_rows + 8), :]
        base = pltpu.roll(wide, tile_rows + 8 - offsets[tile] % 8, 0)[:tile_rows]
        expand = [
            jnp.dot(
                shrink[:, which * half : (which + 1) * half],
                ups[tile, which],
                preferred_element_type=jnp.float32,
            )
            for which in range(2)
        ]
        value = jnp.where(alive, base + jnp.concatenate(expand, axis=1), 0.0)
        out[rows] = value.astype(out.dtype).reshape(tile_rows, 2, width)

    for i in range(per_step):
        tile = t * per_step + i
        rows = slice(i * tile_rows, (i + 1) * tile_rows)
        pltpu.make_async_copy(pools[0].at[0], ups.at[tile], sems.at[tile]).wait()
        pl.when(over)(functools.partial(put, tile, held, rows))
        pl.when(jnp.logical_not(over))(functools.partial(put, tile, base, rows))


def finish(offsets, live, kind, places, totals, rest, parts, pools):
    tiles = offsets.shape[0]
    rows, columns = parts[0].shape
    tile_rows = rows // tiles
    width = totals.shape[1] // 2
    per_step = 2 if tiles % 2 == 0 else 1
    return pl.pallas_call(
        functools.partial(finish_kernel, len(pools), len(parts)),
        out_shape=jax.ShapeDtypeStruct((rows, 2, width), jnp.bfloat16),
        grid_spec=pltpu.PrefetchScalarGridSpec(
            num_scalar_prefetch=4,
            grid=(tiles // per_step,),
            in_specs=[
                pl.BlockSpec(totals.shape, lambda t, *s: (0, 0)),
                pl.BlockSpec(memory_space=pltpu.HBM),
            ]
            + [pl.BlockSpec(memory_space=pltpu.HBM)] * (len(parts) + len(pools)),
            out_specs=pl.BlockSpec((per_step * tile_rows, 2, width), lambda t, *s: (t, 0, 0)),
            scratch_shapes=[
                pltpu.VMEM((rows + tile_rows, 2 * width), jnp.float32),
                pltpu.VMEM((tiles,) + pools[0].shape[1:], pools[0].dtype),
                pltpu.VMEM((len(parts), rows, columns), parts[0].dtype),
                pltpu.SemaphoreType.DMA((tiles,)),
                pltpu.SemaphoreType.DMA((len(parts),)),
                pltpu.SemaphoreType.DMA,
            ],
        ),
        compiler_params=pltpu.CompilerParams(vmem_limit_bytes=48 << 20),
    )(offsets, live, kind, places, totals, rest, *parts, *pools)


def on_device(
    input_rows,
    key_value_weight,
    adapter_down_weight,
    adapter_up_weight,
    tile_page_index,
    tile_live_rows,
):
    groups = lax.axis_size("groups")
    ranks = lax.axis_size("dp")
    shares = lax.axis_size("tensor")
    group = lax.axis_index("groups")
    rank = lax.axis_index("dp")
    share = lax.axis_index("tensor")
    chips = ranks // 2
    chip, core = rank // 2, rank % 2
    tiles = tile_live_rows.shape[0]
    local_pages = adapter_down_weight.shape[0]
    chip_pages = 2 * local_pages
    capacity = max(2, (2 * tiles + ranks - 1) // ranks)
    most_slots = 2 * capacity
    rows, features = input_rows.shape
    tile_rows = rows // tiles
    column_width = key_value_weight.shape[2]
    half = adapter_down_weight.shape[2] // 2

    columns = 2 * column_width
    plane = groups * ranks
    part = features // plane

    line = []

    def ready(value):
        return after(value, line[-1]) if line else value

    def mark(value):
        line.append(jax.tree.leaves(value)[0])
        return value

    def wait(value):
        return mark(ready(value))

    mate_up = flip(adapter_up_weight, "dp", ranks, 1)
    mate_down = flip(adapter_down_weight, "dp", ranks, 1)
    mate_rows = flip(input_rows, "dp", ranks, 1)

    steps = [("dp", ranks, m, (rank // m) % 2) for m in bits(ranks, 2)]
    steps += [("groups", groups, m, (group // m) % 2) for m in bits(groups)]
    steps += [("dp", ranks, 1, core)]
    over_chips = len(bits(ranks, 2))
    last_step = len(steps) - 1
    spot = sum(bit << i for i, (_, _, _, bit) in enumerate(steps))
    turns = list(range(shares - 1, 0, -1))
    order = spot ^ jnp.arange(plane, dtype=jnp.int32)
    entries = [(turns[0], 0)] + [(k, i) for k in turns[1:] for i in range(chips)]
    starts = (share ^ jnp.array([k for k, _ in entries], jnp.int32)) * plane + (
        spot ^ jnp.array([i for _, i in entries], jnp.int32)
    )
    piece = lax.dynamic_slice_in_dim(
        key_value_weight, (share ^ turns[0]) * features + spot * part, part, 0
    )
    piece = mark(piece.reshape(part, columns))
    weights = {turns[0]: flip(piece, "tensor", shares, turns[0])}
    for k in turns[1:]:
        count = chips
        piece = mark(
            side_by_side(starts, ready(key_value_weight), part, entries.index((k, 0)), count)
        )[0]
        weights[k] = piece.reshape(count * part, columns)

    moving = {}

    def begin(key, step):
        axis, size, m, _ = steps[step]
        moving[key, step] = flip(weights[key], axis, size, m)

    def end(key, step):
        got = wait(moving.pop((key, step)))
        weights[key] = mark(jnp.concatenate([weights[key], got]))

    def go_on(key):
        got = wait(moving.pop((key, last_step - 1)))
        axis, size, m, _ = steps[last_step]
        gathered[key] = [weights[key], got] + [flip(v, axis, size, m) for v in (weights[key], got)]

    def get_all(key):
        gathered[key] = gathered[key][:2] + [wait(value) for value in gathered[key][2:]]
        return gathered[key]

    gathered = {}
    arrived = {}

    def lowest(k):
        return k & -k if k else shares

    def take(k, arrived):
        return [arrived.pop(k + m) for m in bits(lowest(k))]

    table = tile_page_index.reshape(chips, 2 * tiles)
    page_range = jnp.arange(ranks * local_pages, dtype=jnp.int32)
    need = jnp.any(table[:, :, None] == page_range[None, None, :], axis=1)
    need = need.reshape(chips, chips, chip_pages)
    position = jnp.cumsum(need.astype(jnp.int32), axis=2) - 1
    usual = -(-5 * most_slots // 8)
    more = -(-6 * most_slots // 8)
    cuts = [0, max(1, 2 * usual // 5), max(2, 4 * usual // 5), usual]
    firsts = [0, 2 * usual, 2 * more, 2 * most_slots]
    most_pages = jnp.max(
        jnp.where(jnp.eye(chips, dtype=jnp.bool_), 0, position[:, :, -1] + 1)
    )
    slot_range = jnp.arange(2 * most_slots, dtype=jnp.int32)
    chip_range = jnp.arange(chip_pages, dtype=jnp.int32)

    offsets = jnp.cumsum(tile_live_rows) - tile_live_rows
    live_total = jnp.sum(tile_live_rows)
    live = jnp.arange(tile_rows, dtype=jnp.int32)[None, :] < tile_live_rows[:, None]
    packed_place = offsets[:, None] + jnp.arange(tile_rows, dtype=jnp.int32)[None, :]
    packed_place = jnp.where(live, packed_place, -1).reshape(rows)
    room = -(-13 * rows // 256) * 16

    listed = []
    for offset in range(1, chips):
        wanted = need[chip ^ offset, chip]
        place = position[chip ^ offset, chip]
        listed.append(
            jnp.sum(
                jnp.where(
                    wanted[None, :] & (place[None, :] == slot_range[:, None]), chip_range[None, :], 0
                ),
                axis=1,
            )
        )
    sent_lists = []
    for offset in range(1, chips):
        halves = [
            listed[offset - 1][low:high].reshape(2, (high - low) // 2)
            for low, high in zip(firsts[:-1], firsts[1:])
        ]
        halves = jnp.concatenate(halves, axis=1)
        sent = jnp.where(core == 0, halves[0], halves[1])
        mine = ((sent // local_pages) == core).astype(jnp.int32)
        at = sent % local_pages
        sent_lists.append((at * mine, at * (1 - mine), mine))

    def locate(pages):
        owner = pages // local_pages
        entry = position[chip, owner // 2, pages % chip_pages]
        return pages % local_pages, owner, (owner // 2) ^ chip, entry

    page_lists = tile_page_index.reshape(ranks, tiles)
    at_home, owner, step, entry = locate(
        jnp.concatenate([page_lists[rank], page_lists[rank ^ 1]])
    )
    kind, places = jnp.where(owner == rank, 0, -1), at_home
    up_kind, up_places = jnp.where(owner == rank, 0, 1), at_home
    for stage in range(3):
        count = (firsts[stage + 1] - firsts[stage]) // 2
        if count == 0:
            continue
        here = (step != 0) & (entry >= firsts[stage])
        sender, at = (entry - firsts[stage]) // count, (entry - firsts[stage]) % count
        far = (sender != core).astype(jnp.int32)
        up_kind = jnp.where(here, 2 + 2 * stage + far, up_kind)
        up_places = jnp.where(here, (step - 1) * count + at, up_places)
        if stage:
            kind = jnp.where(here, (len(cuts) - 1) * (chips - 1) + stage, kind)
            places = jnp.where(here, (step - 1) * count + at, places)
        else:
            for offset in range(1, chips):
                for i in range(len(cuts) - 1):
                    chosen = here & (step == offset) & (at >= cuts[i])
                    kind = jnp.where(chosen, i * (chips - 1) + offset, kind)
                    places = jnp.where(chosen, at - cuts[i], places)
        kind = jnp.where(here & (far == 1), -1, kind)
    up_kind = up_kind[:tiles].astype(jnp.int32)
    up_places = up_places[:tiles].astype(jnp.int32)
    kind, places = kind.astype(jnp.int32), places.astype(jnp.int32)

    first, direct = turns[0], turns[-1]
    crossing = {}
    shared = {}

    def cross(i):
        for offset in range(1, chips):
            crossing[offset, i] = flip(ready(picked[offset - 1][i]), "dp", ranks, 2 * offset)

    def share_pages(i):
        shared[i] = [wait(crossing[offset, i]) for offset in range(1, chips)]

    def product(k):
        added = [wait(value) for value in take(k, arrived)]
        sent = mark(multiply(ready(aside), gathered[k], added, jnp.bfloat16))
        arrived[k] = flip(sent, "tensor", shares, lowest(k))

    def hold(k):
        arrived[k] = wait(arrived[k])

    mate_up = wait(mate_up)
    weights[first] = wait(weights[first])
    begin(first, 0)
    for k in turns[1:-1]:
        weights[k] = flip(ready(weights[k]), "tensor", shares, k)
    weights[direct] = flip(ready(weights[direct]), "tensor", shares, direct)
    mate_down = wait(mate_down)
    mate_rows = wait(mate_rows)
    picked = [
        mark(
            pick_pages(
                lists, 0, cuts, adapter_down_weight, ready(mate_down), adapter_up_weight, mate_up
            )
        )
        for lists in sent_lists
    ]
    cross(0)
    for value in (kind, places, up_kind, up_places):
        mark(value)
    for step in range(over_chips):
        end(first, step)
        begin(first, step + 1)
    packed, aside = pack(packed_place, ready(input_rows), order, part, 0, room)
    mark(aside)
    for k in turns[1:-1]:
        weights[k] = wait(weights[k])
        begin(k, last_step - 1)
    weights[direct] = wait(weights[direct])
    begin(direct, last_step - 1)
    go_on(first)
    get_all(first)
    product(first)
    share_pages(0)
    cross(1)
    cross(2)
    for k in turns[1:-1]:
        go_on(k)
    go_on(direct)
    for k in turns[1:-1]:
        get_all(k)
    values = {
        k: mark(multiply(ready(aside), gathered[k], [], jnp.float32)) for k in turns[1:-1]
    }
    hold(first)
    for k in turns[1:-1]:
        added = [wait(value) for value in take(k, arrived)]
        sent = mark(add_up([values[k]] + added, jnp.bfloat16))
        arrived[k] = flip(sent, "tensor", shares, lowest(k))
    get_all(direct)
    product(direct)
    share_pages(1)
    up_pools = [adapter_up_weight, mate_up]
    more_pools = []
    for stage in (1, 2):

        def send_more(sources):
            low, count = firsts[stage] // 2, (firsts[stage + 1] - firsts[stage]) // 2
            got = []
            for offset in range(1, chips):
                down, up = pick_pages(sent_lists[offset - 1], low, [0, count], *sources)
                got.append((flip(down, "dp", ranks, 2 * offset), flip(up, "dp", ranks, 2 * offset)))
            down = jnp.concatenate([pair[0] for pair in got])
            up = jnp.concatenate([pair[1] for pair in got])
            return down, up, flip(up, "dp", ranks, 1)

        def send_none(sources):
            own_down, _, own_up, _ = sources
            count = (chips - 1) * (firsts[stage + 1] - firsts[stage]) // 2
            down = jax.ShapeDtypeStruct((count,) + own_down.shape[1:], own_down.dtype)
            up = jax.ShapeDtypeStruct((count,) + own_up.shape[1:], own_up.dtype)
            return tuple(blank(down, up, up))

        if firsts[stage + 1] > firsts[stage]:
            near, near_up, far_up = lax.cond(
                most_pages > firsts[stage],
                send_more,
                send_none,
                (ready(adapter_down_weight), mate_down, adapter_up_weight, mate_up),
            )
            more_pools.append(near)
            up_pools += [near_up, far_up]

    near_ups = [
        flip(ready(up), "dp", ranks, 2 * (i + 1)) for i, (*_, up) in enumerate(picked)
    ]
    share_pages(2)
    at = share * plane + jnp.arange(plane, dtype=jnp.int32)
    own = mark(side_by_side(at, ready(key_value_weight), part, 0, plane)[0])
    own = own.reshape(features, columns)
    pools = [adapter_down_weight] + sum((shared[i] for i in range(3)), []) + more_pools
    shrink, mate_shrink = mark(
        tile_shrink(kind, places, ready(input_rows), mate_rows, pools, tiles)
    )
    mate_shrink = flip(mate_shrink, "dp", ranks, 1)
    parts = [mark(shrink + wait(mate_shrink))]
    parts.append(flip(parts[0], "tensor", shares, 1))
    usual_up = jnp.concatenate([wait(up) for up in near_ups])
    usual_ups = [usual_up, flip(usual_up, "dp", ranks, 1)]
    for k in turns[1:-1]:
        if k in arrived:
            hold(k)
    arrived[direct] = wait(arrived[direct])
    parts[-1] = wait(parts[-1])
    later = bits(shares, 2)
    for m in later:
        sent = sum(value.astype(jnp.float32) for value in parts).astype(jnp.bfloat16)
        parts.append(flip(mark(sent), "tensor", shares, m))
        if m != later[-1]:
            parts[-1] = wait(parts[-1])
    final = [wait(value) for value in take(0, arrived)]
    totals = mark(
        multiply(ready(packed), [own], final, jnp.float32, rows - room + tile_rows)
    )
    up_pools[2:2] = usual_ups
    parts[-1] = wait(parts[-1])

    def project_rest(operands):
        x, gathered, own = operands
        packed, aside = pack(packed_place, x, order, part, room, rows)
        arrived = {}
        for k in turns:
            sent = multiply(aside, gathered[k], take(k, arrived), jnp.bfloat16)
            arrived[k] = flip(sent, "tensor", shares, lowest(k))
        return multiply(packed, [own], take(0, arrived), jnp.float32)

    rest_shape = jax.ShapeDtypeStruct((rows - room, columns), jnp.float32)
    rest = lax.cond(
        live_total > room,
        project_rest,
        lambda operands: blank(rest_shape)[0],
        (input_rows, gathered, own),
    )
    return finish(
        offsets,
        tile_live_rows,
        up_kind,
        up_places,
        totals,
        rest,
        parts,
        up_pools,
    )


def solution(mesh):
    return jax.shard_map(
        on_device,
        mesh=mesh,
        in_specs=(
            P(("groups", "dp"), "tensor"),
            P(None, None, "tensor"),
            P("dp", "tensor", None),
            P("dp", None, None, "tensor"),
            P("groups"),
            P(("groups", "dp")),
        ),
        out_specs=P(("groups", "dp"), None, "tensor"),
        check_vma=False,
    )
```

```python
import functools

import jax
import jax.numpy as jnp
from jax import lax
from jax.experimental import pallas as pl
from jax.experimental.pallas import tpu as pltpu
from jax.sharding import PartitionSpec as P


def flip(x, axis, size, mask):
    return lax.ppermute(x, axis, [(i, i ^ mask) for i in range(size)])


def bits(size, first=1):
    out = []
    while first < size:
        out.append(first)
        first *= 2
    return out


def after(value, *others):
    return lax.optimization_barrier((value,) + others)[0]


def pick_kernel(low, cuts, own_at, mate_at, mine, own, mate, own_up, mate_up, *refs):
    *downs, up, sems = refs
    moves = []
    for j in range(cuts[-1]):
        chunk = sum(j >= cut for cut in cuts[1:])
        for place, out, one, other in (
            (0, downs[chunk].at[j - cuts[chunk]], own, mate),
            (1, up.at[j], own_up, mate_up),
        ):
            sem = sems.at[2 * j + place]
            from_own = pltpu.make_async_copy(one.at[own_at[low + j]], out, sem)
            from_mate = pltpu.make_async_copy(other.at[mate_at[low + j]], out, sem)
            pl.when(mine[low + j] == 1)(from_own.start)
            pl.when(mine[low + j] != 1)(from_mate.start)
            moves.append(from_own)
    for move in moves:
        move.wait()


def pick_pages(lists, low, cuts, own, mate, own_up, mate_up):
    counts = [last - first for first, last in zip(cuts[:-1], cuts[1:])]
    return pl.pallas_call(
        functools.partial(pick_kernel, low, cuts),
        out_shape=[jax.ShapeDtypeStruct((count,) + own.shape[1:], own.dtype) for count in counts]
        + [jax.ShapeDtypeStruct((cuts[-1],) + own_up.shape[1:], own_up.dtype)],
        grid_spec=pltpu.PrefetchScalarGridSpec(
            num_scalar_prefetch=3,
            grid=(1,),
            in_specs=[pl.BlockSpec(memory_space=pltpu.HBM)] * 4,
            out_specs=[pl.BlockSpec((count,) + own.shape[1:], lambda i, *s: (0, 0, 0)) for count in counts]
            + [pl.BlockSpec((cuts[-1],) + own_up.shape[1:], lambda i, *s: (0, 0, 0, 0))],
            scratch_shapes=[pltpu.SemaphoreType.DMA((2 * cuts[-1],))],
        ),
        compiler_params=pltpu.CompilerParams(vmem_limit_bytes=32 << 20),
    )(*lists, own, mate, own_up, mate_up)


def blank(*shapes):
    return pl.pallas_call(
        lambda *refs: None,
        out_shape=list(shapes),
        out_specs=[pl.BlockSpec(memory_space=pltpu.HBM)] * len(shapes),
    )()


def side_kernel(weight, out):
    out[0] = weight[...].reshape(out.shape[1:])


def side_by_side(at, weight, part, low, count):
    _, two, width = weight.shape
    return pl.pallas_call(
        lambda at, *refs: side_kernel(*refs),
        out_shape=[jax.ShapeDtypeStruct((count, part, two * width), weight.dtype)],
        grid_spec=pltpu.PrefetchScalarGridSpec(
            num_scalar_prefetch=1,
            grid=(count,),
            in_specs=[pl.BlockSpec((part, two, width), lambda j, at: (at[low + j], 0, 0))],
            out_specs=[pl.BlockSpec((1, part, two * width), lambda j, at: (j, 0, 0))],
        ),
    )(at, weight)


def pack_kernel(first, at, place, x, straight, aside, picks):
    @pl.when(pl.program_id(0) == 0)
    def _():
        row = first + lax.broadcasted_iota(jnp.int32, picks.shape, 0)
        picks[...] = jnp.where(place[...] == row, 1.0, 0.0).astype(picks.dtype)

    packed = jnp.dot(picks[...], x[...], preferred_element_type=jnp.float32).astype(x.dtype)
    straight[...] = packed
    aside[...] = packed


def pack(place, x, at, part, first, last):
    rows, features = x.shape
    count = last - first
    if part % 128:
        pick = place[None, :] == jnp.arange(first, last, dtype=jnp.int32)[:, None]
        packed = jnp.dot(pick.astype(x.dtype), x, preferred_element_type=jnp.float32).astype(x.dtype)
        return packed, packed.reshape(count, -1, part)[:, at].reshape(count, features)
    return pl.pallas_call(
        functools.partial(pack_kernel, first),
        out_shape=[jax.ShapeDtypeStruct((count, features), x.dtype)] * 2,
        grid_spec=pltpu.PrefetchScalarGridSpec(
            num_scalar_prefetch=1,
            grid=(features // part,),
            in_specs=[
                pl.BlockSpec((1, rows), lambda j, at: (0, 0)),
                pl.BlockSpec((rows, part), lambda j, at: (0, j)),
            ],
            out_specs=[
                pl.BlockSpec((count, part), lambda j, at: (0, j)),
                pl.BlockSpec((count, part), lambda j, at: (0, at[j])),
            ],
            scratch_shapes=[pltpu.VMEM((count, rows), x.dtype)],
        ),
        compiler_params=pltpu.CompilerParams(vmem_limit_bytes=32 << 20),
    )(at, place.reshape(1, rows), x)


def add_up_kernel(*refs):
    total = refs[0][...].astype(jnp.float32)
    for ref in refs[1:-1]:
        total = total + ref[...].astype(jnp.float32)
    refs[-1][...] = total.astype(refs[-1].dtype)


def add_up(values, dtype):
    rows, width = values[0].shape
    block = rows // 2 if rows % 32 == 0 else rows
    piece = pl.BlockSpec((block, width), lambda j: (j, 0))
    return pl.pallas_call(
        add_up_kernel,
        out_shape=jax.ShapeDtypeStruct((rows, width), dtype),
        grid=(rows // block,),
        in_specs=[piece] * len(values),
        out_specs=piece,
        compiler_params=pltpu.CompilerParams(vmem_limit_bytes=32 << 20),
    )(*values)


def multiply_kernel(parts, adds, x, *refs):
    weights, added, refs = refs[:parts], refs[parts : parts + adds], refs[parts + adds :]
    out = refs[0]
    j = pl.program_id(0)
    block = x.shape[0]
    moves = []
    if adds:
        added_in, sems = refs[1:]
        moves = [
            pltpu.make_async_copy(ref, added_in.at[i], sems.at[i]) for i, ref in enumerate(added)
        ]

    @pl.when(j == 0)
    def _():
        for move in moves:
            move.start()

    total, low = None, 0
    for weight in weights:
        high = low + weight.shape[0]
        piece = jnp.dot(x[:, low:high], weight[...], preferred_element_type=jnp.float32)
        total, low = piece if total is None else total + piece, high

    @pl.when(j == 0)
    def _():
        for move in moves:
            move.wait()

    for i in range(adds):
        rows = pl.ds(pl.multiple_of(j * block, block), block)
        total = total + added_in[i, rows, :].astype(jnp.float32)
    out[...] = total.astype(out.dtype)


def multiply(x, weights, added, dtype, spare=0):
    rows, features = x.shape
    block = rows // 2 if rows % 32 == 0 else rows
    width = weights[0].shape[1]
    scratch = []
    if added:
        scratch = [
            pltpu.VMEM((len(added), rows, width), added[0].dtype),
            pltpu.SemaphoreType.DMA((len(added),)),
        ]
    return pl.pallas_call(
        functools.partial(multiply_kernel, len(weights), len(added)),
        out_shape=jax.ShapeDtypeStruct((rows + spare, width), dtype),
        grid=(rows // block,),
        in_specs=[pl.BlockSpec((block, features), lambda j: (j, 0))]
        + [pl.BlockSpec(weight.shape, lambda j: (0, 0)) for weight in weights]
        + [pl.BlockSpec(memory_space=pl.ANY)] * len(added),
        out_specs=pl.BlockSpec((block, width), lambda j: (j, 0)),
        scratch_shapes=scratch,
        compiler_params=pltpu.CompilerParams(vmem_limit_bytes=40 << 20),
    )(x, *weights, *added)


def shrink_kernel(count, tiles, kind, places, *refs):
    (own_x, mate_x), pools, outs = refs[:2], refs[2 : 2 + count], refs[2 + count : 4 + count]
    rows_in, pages, row_sems, sems = refs[4 + count :]
    tile_rows = outs[0].shape[0] // tiles
    for i in range(2 * tiles):
        rows = pl.ds(i % tiles * tile_rows, tile_rows)
        x = own_x if i < tiles else mate_x
        for number, pool in enumerate(pools):
            move = pltpu.make_async_copy(pool.at[places[i]], pages.at[i], sems.at[i])
            pl.when(kind[i] == number)(move.start)
        move = pltpu.make_async_copy(x.at[rows], rows_in.at[i], row_sems.at[i])
        pl.when(kind[i] >= 0)(move.start)
    for i in range(2 * tiles):
        rows = pl.ds(i % tiles * tile_rows, tile_rows)
        x, out = (own_x, outs[0]) if i < tiles else (mate_x, outs[1])

        @pl.when(kind[i] >= 0)
        def _(i=i, rows=rows, x=x, out=out):
            pltpu.make_async_copy(pools[0].at[0], pages.at[i], sems.at[i]).wait()
            pltpu.make_async_copy(x.at[rows], rows_in.at[i], row_sems.at[i]).wait()
            out[rows, :] = jnp.dot(
                rows_in[i], pages[i], preferred_element_type=jnp.float32
            ).astype(out.dtype)

        @pl.when(kind[i] < 0)
        def _(rows=rows, out=out):
            out[rows, :] = jnp.zeros((tile_rows, out.shape[1]), out.dtype)


def tile_shrink(kind, places, own_x, mate_x, pools, tiles):
    features, columns = pools[0].shape[1:]
    rows = own_x.shape[0]
    out = pl.BlockSpec((rows, columns), lambda i, *s: (0, 0))
    return pl.pallas_call(
        functools.partial(shrink_kernel, len(pools), tiles),
        out_shape=[jax.ShapeDtypeStruct((rows, columns), jnp.bfloat16)] * 2,
        grid_spec=pltpu.PrefetchScalarGridSpec(
            num_scalar_prefetch=2,
            grid=(1,),
            in_specs=[pl.BlockSpec(memory_space=pltpu.HBM)] * (2 + len(pools)),
            out_specs=[out, out],
            scratch_shapes=[
                pltpu.VMEM((2 * tiles, rows // tiles, features), own_x.dtype),
                pltpu.VMEM((2 * tiles, features, columns), pools[0].dtype),
                pltpu.SemaphoreType.DMA((2 * tiles,)),
                pltpu.SemaphoreType.DMA((2 * tiles,)),
            ],
        ),
        compiler_params=pltpu.CompilerParams(vmem_limit_bytes=48 << 20),
    )(kind, places, own_x, mate_x, *pools)


def finish_kernel(count, terms, offsets, live, kind, places, *refs):
    base, more = refs[:2]
    parts, pools = refs[2 : 2 + terms], refs[2 + terms : 2 + terms + count]
    out, held, ups, terms_in, sems, term_sems, more_sem = refs[2 + terms + count :]
    t = pl.program_id(0)
    tiles = ups.shape[0]
    tile_rows, width = parts[0].shape[0] // tiles, out.shape[2]
    per_step = out.shape[0] // tile_rows
    half = ups.shape[2]
    rest = more.shape[0]
    rows = held.shape[0] - tile_rows
    room = rows - rest
    over = offsets[tiles - 1] + live[tiles - 1] > room

    part_moves = [
        pltpu.make_async_copy(part, terms_in.at[i], term_sems.at[i]) for i, part in enumerate(parts)
    ]

    @pl.when(t == 0)
    def _():
        for move in part_moves:
            move.start()
        for tile in range(tiles):
            for number, pool in enumerate(pools):
                move = pltpu.make_async_copy(pool.at[places[tile]], ups.at[tile], sems.at[tile])
                pl.when(kind[tile] == number)(move.start)

    @pl.when((t == 0) & over)
    def _():
        move = pltpu.make_async_copy(more, held.at[pl.ds(room, rest)], more_sem)
        move.start()
        held[:room] = base[:room]
        held[rows:] = jnp.zeros((tile_rows, 2 * width), jnp.float32)
        move.wait()

    @pl.when(t == 0)
    def _():
        for move in part_moves:
            move.wait()

    def put(tile, source, rows):
        low = pl.multiple_of((offsets[tile] // 8) * 8, 8)
        alive = lax.broadcasted_iota(jnp.int32, (tile_rows, 2 * width), 0) < live[tile]
        span = pl.ds(pl.multiple_of(tile * tile_rows, tile_rows), tile_rows)
        shrink = terms_in[0, span, :].astype(jnp.float32)
        for i in range(1, terms):
            shrink = shrink + terms_in[i, span, :].astype(jnp.float32)
        shrink = shrink.astype(jnp.bfloat16)
        wide = source[pl.ds(low, tile_rows + 8), :]
        base = pltpu.roll(wide, tile_rows + 8 - offsets[tile] % 8, 0)[:tile_rows]
        expand = [
            jnp.dot(
                shrink[:, which * half : (which + 1) * half],
                ups[tile, which],
                preferred_element_type=jnp.float32,
            )
            for which in range(2)
        ]
        value = jnp.where(alive, base + jnp.concatenate(expand, axis=1), 0.0)
        out[rows] = value.astype(out.dtype).reshape(tile_rows, 2, width)

    for i in range(per_step):
        tile = t * per_step + i
        rows = slice(i * tile_rows, (i + 1) * tile_rows)
        pltpu.make_async_copy(pools[0].at[0], ups.at[tile], sems.at[tile]).wait()
        pl.when(over)(functools.partial(put, tile, held, rows))
        pl.when(jnp.logical_not(over))(functools.partial(put, tile, base, rows))


def finish(offsets, live, kind, places, totals, rest, parts, pools):
    tiles = offsets.shape[0]
    rows, columns = parts[0].shape
    tile_rows = rows // tiles
    width = totals.shape[1] // 2
    per_step = 2 if tiles % 2 == 0 else 1
    return pl.pallas_call(
        functools.partial(finish_kernel, len(pools), len(parts)),
        out_shape=jax.ShapeDtypeStruct((rows, 2, width), jnp.bfloat16),
        grid_spec=pltpu.PrefetchScalarGridSpec(
            num_scalar_prefetch=4,
            grid=(tiles // per_step,),
            in_specs=[
                pl.BlockSpec(totals.shape, lambda t, *s: (0, 0)),
                pl.BlockSpec(memory_space=pltpu.HBM),
            ]
            + [pl.BlockSpec(memory_space=pltpu.HBM)] * (len(parts) + len(pools)),
            out_specs=pl.BlockSpec((per_step * tile_rows, 2, width), lambda t, *s: (t, 0, 0)),
            scratch_shapes=[
                pltpu.VMEM((rows + tile_rows, 2 * width), jnp.float32),
                pltpu.VMEM((tiles,) + pools[0].shape[1:], pools[0].dtype),
                pltpu.VMEM((len(parts), rows, columns), parts[0].dtype),
                pltpu.SemaphoreType.DMA((tiles,)),
                pltpu.SemaphoreType.DMA((len(parts),)),
                pltpu.SemaphoreType.DMA,
            ],
        ),
        compiler_params=pltpu.CompilerParams(vmem_limit_bytes=48 << 20),
    )(offsets, live, kind, places, totals, rest, *parts, *pools)


def on_device(
    input_rows,
    key_value_weight,
    adapter_down_weight,
    adapter_up_weight,
    tile_page_index,
    tile_live_rows,
):
    groups = lax.axis_size("groups")
    ranks = lax.axis_size("dp")
    shares = lax.axis_size("tensor")
    group = lax.axis_index("groups")
    rank = lax.axis_index("dp")
    share = lax.axis_index("tensor")
    chips = ranks // 2
    chip, core = rank // 2, rank % 2
    tiles = tile_live_rows.shape[0]
    local_pages = adapter_down_weight.shape[0]
    chip_pages = 2 * local_pages
    capacity = max(2, (2 * tiles + ranks - 1) // ranks)
    most_slots = 2 * capacity
    rows, features = input_rows.shape
    tile_rows = rows // tiles
    column_width = key_value_weight.shape[2]
    half = adapter_down_weight.shape[2] // 2

    columns = 2 * column_width
    plane = groups * ranks
    part = features // plane

    line = []

    def ready(value):
        return after(value, line[-1]) if line else value

    def mark(value):
        line.append(jax.tree.leaves(value)[0])
        return value

    def wait(value):
        return mark(ready(value))

    mate_up = flip(adapter_up_weight, "dp", ranks, 1)
    mate_down = flip(adapter_down_weight, "dp", ranks, 1)
    mate_rows = flip(input_rows, "dp", ranks, 1)

    steps = [("dp", ranks, m, (rank // m) % 2) for m in bits(ranks, 2)]
    steps += [("groups", groups, m, (group // m) % 2) for m in bits(groups)]
    steps += [("dp", ranks, 1, core)]
    over_chips = len(bits(ranks, 2))
    last_step = len(steps) - 1
    spot = sum(bit << i for i, (_, _, _, bit) in enumerate(steps))
    turns = list(range(shares - 1, 0, -1))
    order = spot ^ jnp.arange(plane, dtype=jnp.int32)
    entries = [(turns[0], 0)] + [(k, i) for k in turns[1:] for i in range(chips)]
    starts = (share ^ jnp.array([k for k, _ in entries], jnp.int32)) * plane + (
        spot ^ jnp.array([i for _, i in entries], jnp.int32)
    )
    piece = lax.dynamic_slice_in_dim(
        key_value_weight, (share ^ turns[0]) * features + spot * part, part, 0
    )
    piece = mark(piece.reshape(part, columns))
    weights = {turns[0]: flip(piece, "tensor", shares, turns[0])}
    for k in turns[1:]:
        count = chips
        piece = mark(
            side_by_side(starts, ready(key_value_weight), part, entries.index((k, 0)), count)
        )[0]
        weights[k] = piece.reshape(count * part, columns)

    moving = {}

    def begin(key, step):
        axis, size, m, _ = steps[step]
        moving[key, step] = flip(weights[key], axis, size, m)

    def end(key, step):
        got = wait(moving.pop((key, step)))
        weights[key] = mark(jnp.concatenate([weights[key], got]))

    def go_on(key):
        got = wait(moving.pop((key, last_step - 1)))
        axis, size, m, _ = steps[last_step]
        gathered[key] = [weights[key], got] + [flip(v, axis, size, m) for v in (weights[key], got)]

    def get_all(key):
        gathered[key] = gathered[key][:2] + [wait(value) for value in gathered[key][2:]]
        return gathered[key]

    gathered = {}
    arrived = {}

    def lowest(k):
        return k & -k if k else shares

    def take(k, arrived):
        return [arrived.pop(k + m) for m in bits(lowest(k))]

    table = tile_page_index.reshape(chips, 2 * tiles)
    page_range = jnp.arange(ranks * local_pages, dtype=jnp.int32)
    need = jnp.any(table[:, :, None] == page_range[None, None, :], axis=1)
    need = need.reshape(chips, chips, chip_pages)
    position = jnp.cumsum(need.astype(jnp.int32), axis=2) - 1
    usual = -(-5 * most_slots // 8)
    more = -(-6 * most_slots // 8)
    cuts = [0, max(1, 2 * usual // 5), max(2, 4 * usual // 5), usual]
    firsts = [0, 2 * usual, 2 * more, 2 * most_slots]
    most_pages = jnp.max(
        jnp.where(jnp.eye(chips, dtype=jnp.bool_), 0, position[:, :, -1] + 1)
    )
    slot_range = jnp.arange(2 * most_slots, dtype=jnp.int32)
    chip_range = jnp.arange(chip_pages, dtype=jnp.int32)

    offsets = jnp.cumsum(tile_live_rows) - tile_live_rows
    live_total = jnp.sum(tile_live_rows)
    live = jnp.arange(tile_rows, dtype=jnp.int32)[None, :] < tile_live_rows[:, None]
    packed_place = offsets[:, None] + jnp.arange(tile_rows, dtype=jnp.int32)[None, :]
    packed_place = jnp.where(live, packed_place, -1).reshape(rows)
    room = -(-13 * rows // 256) * 16

    listed = []
    for offset in range(1, chips):
        wanted = need[chip ^ offset, chip]
        place = position[chip ^ offset, chip]
        listed.append(
            jnp.sum(
                jnp.where(
                    wanted[None, :] & (place[None, :] == slot_range[:, None]), chip_range[None, :], 0
                ),
                axis=1,
            )
        )
    sent_lists = []
    for offset in range(1, chips):
        halves = [
            listed[offset - 1][low:high].reshape(2, (high - low) // 2)
            for low, high in zip(firsts[:-1], firsts[1:])
        ]
        halves = jnp.concatenate(halves, axis=1)
        sent = jnp.where(core == 0, halves[0], halves[1])
        mine = ((sent // local_pages) == core).astype(jnp.int32)
        at = sent % local_pages
        sent_lists.append((at * mine, at * (1 - mine), mine))

    def locate(pages):
        owner = pages // local_pages
        entry = position[chip, owner // 2, pages % chip_pages]
        return pages % local_pages, owner, (owner // 2) ^ chip, entry

    page_lists = tile_page_index.reshape(ranks, tiles)
    at_home, owner, step, entry = locate(
        jnp.concatenate([page_lists[rank], page_lists[rank ^ 1]])
    )
    kind, places = jnp.where(owner == rank, 0, -1), at_home
    up_kind, up_places = jnp.where(owner == rank, 0, 1), at_home
    for stage in range(3):
        count = (firsts[stage + 1] - firsts[stage]) // 2
        if count == 0:
            continue
        here = (step != 0) & (entry >= firsts[stage])
        sender, at = (entry - firsts[stage]) // count, (entry - firsts[stage]) % count
        far = (sender != core).astype(jnp.int32)
        up_kind = jnp.where(here, 2 + 2 * stage + far, up_kind)
        up_places = jnp.where(here, (step - 1) * count + at, up_places)
        if stage:
            kind = jnp.where(here, (len(cuts) - 1) * (chips - 1) + stage, kind)
            places = jnp.where(here, (step - 1) * count + at, places)
        else:
            for offset in range(1, chips):
                for i in range(len(cuts) - 1):
                    chosen = here & (step == offset) & (at >= cuts[i])
                    kind = jnp.where(chosen, i * (chips - 1) + offset, kind)
                    places = jnp.where(chosen, at - cuts[i], places)
        kind = jnp.where(here & (far == 1), -1, kind)
    up_kind = up_kind[:tiles].astype(jnp.int32)
    up_places = up_places[:tiles].astype(jnp.int32)
    kind, places = kind.astype(jnp.int32), places.astype(jnp.int32)

    first, direct = turns[0], turns[-1]
    crossing = {}
    shared = {}

    def cross(i):
        for offset in range(1, chips):
            crossing[offset, i] = flip(ready(picked[offset - 1][i]), "dp", ranks, 2 * offset)

    def share_pages(i):
        shared[i] = [wait(crossing[offset, i]) for offset in range(1, chips)]

    def product(k):
        added = [wait(value) for value in take(k, arrived)]
        sent = mark(multiply(ready(aside), gathered[k], added, jnp.bfloat16))
        arrived[k] = flip(sent, "tensor", shares, lowest(k))

    def hold(k):
        arrived[k] = wait(arrived[k])

    mate_up = wait(mate_up)
    weights[first] = wait(weights[first])
    begin(first, 0)
    for k in turns[1:-1]:
        weights[k] = flip(ready(weights[k]), "tensor", shares, k)
    weights[direct] = flip(ready(weights[direct]), "tensor", shares, direct)
    mate_down = wait(mate_down)
    mate_rows = wait(mate_rows)
    picked = [
        mark(
            pick_pages(
                lists, 0, cuts, adapter_down_weight, ready(mate_down), adapter_up_weight, mate_up
            )
        )
        for lists in sent_lists
    ]
    cross(0)
    for value in (kind, places, up_kind, up_places):
        mark(value)
    for step in range(over_chips):
        end(first, step)
        begin(first, step + 1)
    packed, aside = pack(packed_place, ready(input_rows), order, part, 0, room)
    mark(aside)
    for k in turns[1:-1]:
        weights[k] = wait(weights[k])
        begin(k, last_step - 1)
    weights[direct] = wait(weights[direct])
    begin(direct, last_step - 1)
    go_on(first)
    get_all(first)
    product(first)
    share_pages(0)
    cross(1)
    cross(2)
    for k in turns[1:-1]:
        go_on(k)
    go_on(direct)
    for k in turns[1:-1]:
        get_all(k)
    values = {
        k: mark(multiply(ready(aside), gathered[k], [], jnp.float32)) for k in turns[1:-1]
    }
    hold(first)
    for k in turns[1:-1]:
        added = [wait(value) for value in take(k, arrived)]
        sent = mark(add_up([values[k]] + added, jnp.bfloat16))
        arrived[k] = flip(sent, "tensor", shares, lowest(k))
    get_all(direct)
    product(direct)
    share_pages(1)
    up_pools = [adapter_up_weight, mate_up]
    more_pools = []
    for stage in (1, 2):

        def send_more(sources):
            low, count = firsts[stage] // 2, (firsts[stage + 1] - firsts[stage]) // 2
            got = []
            for offset in range(1, chips):
                down, up = pick_pages(sent_lists[offset - 1], low, [0, count], *sources)
                got.append((flip(down, "dp", ranks, 2 * offset), flip(up, "dp", ranks, 2 * offset)))
            down = jnp.concatenate([pair[0] for pair in got])
            up = jnp.concatenate([pair[1] for pair in got])
            return down, up, flip(up, "dp", ranks, 1)

        def send_none(sources):
            own_down, _, own_up, _ = sources
            count = (chips - 1) * (firsts[stage + 1] - firsts[stage]) // 2
            down = jax.ShapeDtypeStruct((count,) + own_down.shape[1:], own_down.dtype)
            up = jax.ShapeDtypeStruct((count,) + own_up.shape[1:], own_up.dtype)
            return tuple(blank(down, up, up))

        if firsts[stage + 1] > firsts[stage]:
            near, near_up, far_up = lax.cond(
                most_pages > firsts[stage],
                send_more,
                send_none,
                (ready(adapter_down_weight), mate_down, adapter_up_weight, mate_up),
            )
            more_pools.append(near)
            up_pools += [near_up, far_up]

    near_ups = [
        flip(ready(up), "dp", ranks, 2 * (i + 1)) for i, (*_, up) in enumerate(picked)
    ]
    at = share * plane + jnp.arange(plane, dtype=jnp.int32)
    own = mark(side_by_side(at, ready(key_value_weight), part, 0, plane)[0])
    own = own.reshape(features, columns)
    share_pages(2)
    pools = [adapter_down_weight] + sum((shared[i] for i in range(3)), []) + more_pools
    shrink, mate_shrink = mark(
        tile_shrink(kind, places, ready(input_rows), mate_rows, pools, tiles)
    )
    mate_shrink = flip(mate_shrink, "dp", ranks, 1)
    parts = [mark(shrink + wait(mate_shrink))]
    parts.append(flip(parts[0], "tensor", shares, 1))
    usual_up = jnp.concatenate([wait(up) for up in near_ups])
    usual_ups = [usual_up, flip(usual_up, "dp", ranks, 1)]
    for k in turns[1:-1]:
        if k in arrived:
            hold(k)
    arrived[direct] = wait(arrived[direct])
    parts[-1] = wait(parts[-1])
    later = bits(shares, 2)
    for m in later:
        sent = sum(value.astype(jnp.float32) for value in parts).astype(jnp.bfloat16)
        parts.append(flip(mark(sent), "tensor", shares, m))
        if m != later[-1]:
            parts[-1] = wait(parts[-1])
    final = [wait(value) for value in take(0, arrived)]
    totals = mark(
        multiply(ready(packed), [own], final, jnp.float32, rows - room + tile_rows)
    )
    up_pools[2:2] = usual_ups
    parts[-1] = wait(parts[-1])

    def project_rest(operands):
        x, gathered, own = operands
        packed, aside = pack(packed_place, x, order, part, room, rows)
        arrived = {}
        for k in turns:
            sent = multiply(aside, gathered[k], take(k, arrived), jnp.bfloat16)
            arrived[k] = flip(sent, "tensor", shares, lowest(k))
        return multiply(packed, [own], take(0, arrived), jnp.float32)

    rest_shape = jax.ShapeDtypeStruct((rows - room, columns), jnp.float32)
    rest = lax.cond(
        live_total > room,
        project_rest,
        lambda operands: blank(rest_shape)[0],
        (input_rows, gathered, own),
    )
    return finish(
        offsets,
        tile_live_rows,
        up_kind,
        up_places,
        totals,
        rest,
        parts,
        up_pools,
    )


def solution(mesh):
    return jax.shard_map(
        on_device,
        mesh=mesh,
        in_specs=(
            P(("groups", "dp"), "tensor"),
            P(None, None, "tensor"),
            P("dp", "tensor", None),
            P("dp", None, None, "tensor"),
            P("groups"),
            P(("groups", "dp")),
        ),
        out_specs=P(("groups", "dp"), None, "tensor"),
        check_vma=False,
    )
```

```python
import functools

import jax
import jax.numpy as jnp
from jax import lax
from jax.experimental import pallas as pl
from jax.experimental.pallas import tpu as pltpu
from jax.sharding import PartitionSpec as P


def flip(x, axis, size, mask):
    return lax.ppermute(x, axis, [(i, i ^ mask) for i in range(size)])


def bits(size, first=1):
    out = []
    while first < size:
        out.append(first)
        first *= 2
    return out


def after(value, *others):
    return lax.optimization_barrier((value,) + others)[0]


def pick_kernel(low, cuts, own_at, mate_at, mine, own, mate, own_up, mate_up, *refs):
    *downs, up, sems = refs
    moves = []
    for j in range(cuts[-1]):
        chunk = sum(j >= cut for cut in cuts[1:])
        for place, out, one, other in (
            (0, downs[chunk].at[j - cuts[chunk]], own, mate),
            (1, up.at[j], own_up, mate_up),
        ):
            sem = sems.at[2 * j + place]
            from_own = pltpu.make_async_copy(one.at[own_at[low + j]], out, sem)
            from_mate = pltpu.make_async_copy(other.at[mate_at[low + j]], out, sem)
            pl.when(mine[low + j] == 1)(from_own.start)
            pl.when(mine[low + j] != 1)(from_mate.start)
            moves.append(from_own)
    for move in moves:
        move.wait()


def pick_pages(lists, low, cuts, own, mate, own_up, mate_up):
    counts = [last - first for first, last in zip(cuts[:-1], cuts[1:])]
    return pl.pallas_call(
        functools.partial(pick_kernel, low, cuts),
        out_shape=[jax.ShapeDtypeStruct((count,) + own.shape[1:], own.dtype) for count in counts]
        + [jax.ShapeDtypeStruct((cuts[-1],) + own_up.shape[1:], own_up.dtype)],
        grid_spec=pltpu.PrefetchScalarGridSpec(
            num_scalar_prefetch=3,
            grid=(1,),
            in_specs=[pl.BlockSpec(memory_space=pltpu.HBM)] * 4,
            out_specs=[pl.BlockSpec((count,) + own.shape[1:], lambda i, *s: (0, 0, 0)) for count in counts]
            + [pl.BlockSpec((cuts[-1],) + own_up.shape[1:], lambda i, *s: (0, 0, 0, 0))],
            scratch_shapes=[pltpu.SemaphoreType.DMA((2 * cuts[-1],))],
        ),
        compiler_params=pltpu.CompilerParams(vmem_limit_bytes=32 << 20),
    )(*lists, own, mate, own_up, mate_up)


def blank(*shapes):
    return pl.pallas_call(
        lambda *refs: None,
        out_shape=list(shapes),
        out_specs=[pl.BlockSpec(memory_space=pltpu.HBM)] * len(shapes),
    )()


def side_kernel(weight, out):
    out[0] = weight[...].reshape(out.shape[1:])


def side_by_side(at, weight, part, low, count):
    _, two, width = weight.shape
    return pl.pallas_call(
        lambda at, *refs: side_kernel(*refs),
        out_shape=[jax.ShapeDtypeStruct((count, part, two * width), weight.dtype)],
        grid_spec=pltpu.PrefetchScalarGridSpec(
            num_scalar_prefetch=1,
            grid=(count,),
            in_specs=[pl.BlockSpec((part, two, width), lambda j, at: (at[low + j], 0, 0))],
            out_specs=[pl.BlockSpec((1, part, two * width), lambda j, at: (j, 0, 0))],
        ),
    )(at, weight)


def pack_kernel(first, at, place, x, straight, aside, picks):
    @pl.when(pl.program_id(0) == 0)
    def _():
        row = first + lax.broadcasted_iota(jnp.int32, picks.shape, 0)
        picks[...] = jnp.where(place[...] == row, 1.0, 0.0).astype(picks.dtype)

    packed = jnp.dot(picks[...], x[...], preferred_element_type=jnp.float32).astype(x.dtype)
    straight[...] = packed
    aside[...] = packed


def pack(place, x, at, part, first, last):
    rows, features = x.shape
    count = last - first
    if part % 128:
        pick = place[None, :] == jnp.arange(first, last, dtype=jnp.int32)[:, None]
        packed = jnp.dot(pick.astype(x.dtype), x, preferred_element_type=jnp.float32).astype(x.dtype)
        return packed, packed.reshape(count, -1, part)[:, at].reshape(count, features)
    return pl.pallas_call(
        functools.partial(pack_kernel, first),
        out_shape=[jax.ShapeDtypeStruct((count, features), x.dtype)] * 2,
        grid_spec=pltpu.PrefetchScalarGridSpec(
            num_scalar_prefetch=1,
            grid=(features // part,),
            in_specs=[
                pl.BlockSpec((1, rows), lambda j, at: (0, 0)),
                pl.BlockSpec((rows, part), lambda j, at: (0, j)),
            ],
            out_specs=[
                pl.BlockSpec((count, part), lambda j, at: (0, j)),
                pl.BlockSpec((count, part), lambda j, at: (0, at[j])),
            ],
            scratch_shapes=[pltpu.VMEM((count, rows), x.dtype)],
        ),
        compiler_params=pltpu.CompilerParams(vmem_limit_bytes=32 << 20),
    )(at, place.reshape(1, rows), x)


def add_up_kernel(*refs):
    total = refs[0][...].astype(jnp.float32)
    for ref in refs[1:-1]:
        total = total + ref[...].astype(jnp.float32)
    refs[-1][...] = total.astype(refs[-1].dtype)


def add_up(values, dtype):
    rows, width = values[0].shape
    block = rows // 2 if rows % 32 == 0 else rows
    piece = pl.BlockSpec((block, width), lambda j: (j, 0))
    return pl.pallas_call(
        add_up_kernel,
        out_shape=jax.ShapeDtypeStruct((rows, width), dtype),
        grid=(rows // block,),
        in_specs=[piece] * len(values),
        out_specs=piece,
        compiler_params=pltpu.CompilerParams(vmem_limit_bytes=32 << 20),
    )(*values)


def multiply_kernel(parts, adds, x, *refs):
    weights, added, refs = refs[:parts], refs[parts : parts + adds], refs[parts + adds :]
    out = refs[0]
    j = pl.program_id(0)
    block = x.shape[0]
    moves = []
    if adds:
        added_in, sems = refs[1:]
        moves = [
            pltpu.make_async_copy(ref, added_in.at[i], sems.at[i]) for i, ref in enumerate(added)
        ]

    @pl.when(j == 0)
    def _():
        for move in moves:
            move.start()

    total, low = None, 0
    for weight in weights:
        high = low + weight.shape[0]
        piece = jnp.dot(x[:, low:high], weight[...], preferred_element_type=jnp.float32)
        total, low = piece if total is None else total + piece, high

    @pl.when(j == 0)
    def _():
        for move in moves:
            move.wait()

    for i in range(adds):
        rows = pl.ds(pl.multiple_of(j * block, block), block)
        total = total + added_in[i, rows, :].astype(jnp.float32)
    out[...] = total.astype(out.dtype)


def multiply(x, weights, added, dtype, spare=0):
    rows, features = x.shape
    block = rows // 2 if rows % 32 == 0 else rows
    width = weights[0].shape[1]
    scratch = []
    if added:
        scratch = [
            pltpu.VMEM((len(added), rows, width), added[0].dtype),
            pltpu.SemaphoreType.DMA((len(added),)),
        ]
    return pl.pallas_call(
        functools.partial(multiply_kernel, len(weights), len(added)),
        out_shape=jax.ShapeDtypeStruct((rows + spare, width), dtype),
        grid=(rows // block,),
        in_specs=[pl.BlockSpec((block, features), lambda j: (j, 0))]
        + [pl.BlockSpec(weight.shape, lambda j: (0, 0)) for weight in weights]
        + [pl.BlockSpec(memory_space=pl.ANY)] * len(added),
        out_specs=pl.BlockSpec((block, width), lambda j: (j, 0)),
        scratch_shapes=scratch,
        compiler_params=pltpu.CompilerParams(vmem_limit_bytes=40 << 20),
    )(x, *weights, *added)


def shrink_kernel(count, tiles, kind, places, *refs):
    (own_x, mate_x), pools, outs = refs[:2], refs[2 : 2 + count], refs[2 + count : 4 + count]
    rows_in, pages, row_sems, sems = refs[4 + count :]
    tile_rows = outs[0].shape[0] // tiles
    for i in range(2 * tiles):
        rows = pl.ds(i % tiles * tile_rows, tile_rows)
        x = own_x if i < tiles else mate_x
        for number, pool in enumerate(pools):
            move = pltpu.make_async_copy(pool.at[places[i]], pages.at[i], sems.at[i])
            pl.when(kind[i] == number)(move.start)
        move = pltpu.make_async_copy(x.at[rows], rows_in.at[i], row_sems.at[i])
        pl.when(kind[i] >= 0)(move.start)
    for i in range(2 * tiles):
        rows = pl.ds(i % tiles * tile_rows, tile_rows)
        x, out = (own_x, outs[0]) if i < tiles else (mate_x, outs[1])

        @pl.when(kind[i] >= 0)
        def _(i=i, rows=rows, x=x, out=out):
            pltpu.make_async_copy(pools[0].at[0], pages.at[i], sems.at[i]).wait()
            pltpu.make_async_copy(x.at[rows], rows_in.at[i], row_sems.at[i]).wait()
            out[rows, :] = jnp.dot(
                rows_in[i], pages[i], preferred_element_type=jnp.float32
            ).astype(out.dtype)

        @pl.when(kind[i] < 0)
        def _(rows=rows, out=out):
            out[rows, :] = jnp.zeros((tile_rows, out.shape[1]), out.dtype)


def tile_shrink(kind, places, own_x, mate_x, pools, tiles):
    features, columns = pools[0].shape[1:]
    rows = own_x.shape[0]
    out = pl.BlockSpec((rows, columns), lambda i, *s: (0, 0))
    return pl.pallas_call(
        functools.partial(shrink_kernel, len(pools), tiles),
        out_shape=[jax.ShapeDtypeStruct((rows, columns), jnp.bfloat16)] * 2,
        grid_spec=pltpu.PrefetchScalarGridSpec(
            num_scalar_prefetch=2,
            grid=(1,),
            in_specs=[pl.BlockSpec(memory_space=pltpu.HBM)] * (2 + len(pools)),
            out_specs=[out, out],
            scratch_shapes=[
                pltpu.VMEM((2 * tiles, rows // tiles, features), own_x.dtype),
                pltpu.VMEM((2 * tiles, features, columns), pools[0].dtype),
                pltpu.SemaphoreType.DMA((2 * tiles,)),
                pltpu.SemaphoreType.DMA((2 * tiles,)),
            ],
        ),
        compiler_params=pltpu.CompilerParams(vmem_limit_bytes=48 << 20),
    )(kind, places, own_x, mate_x, *pools)


def finish_kernel(count, terms, offsets, live, kind, places, *refs):
    base, more = refs[:2]
    parts, pools = refs[2 : 2 + terms], refs[2 + terms : 2 + terms + count]
    out, held, ups, terms_in, sems, term_sems, more_sem = refs[2 + terms + count :]
    t = pl.program_id(0)
    tiles = ups.shape[0]
    tile_rows, width = parts[0].shape[0] // tiles, out.shape[2]
    per_step = out.shape[0] // tile_rows
    half = ups.shape[2]
    rest = more.shape[0]
    rows = held.shape[0] - tile_rows
    room = rows - rest
    over = offsets[tiles - 1] + live[tiles - 1] > room

    part_moves = [
        pltpu.make_async_copy(part, terms_in.at[i], term_sems.at[i]) for i, part in enumerate(parts)
    ]

    @pl.when(t == 0)
    def _():
        for move in part_moves:
            move.start()
        for tile in range(tiles):
            for number, pool in enumerate(pools):
                move = pltpu.make_async_copy(pool.at[places[tile]], ups.at[tile], sems.at[tile])
                pl.when(kind[tile] == number)(move.start)

    @pl.when((t == 0) & over)
    def _():
        move = pltpu.make_async_copy(more, held.at[pl.ds(room, rest)], more_sem)
        move.start()
        held[:room] = base[:room]
        held[rows:] = jnp.zeros((tile_rows, 2 * width), jnp.float32)
        move.wait()

    @pl.when(t == 0)
    def _():
        for move in part_moves:
            move.wait()

    def put(tile, source, rows):
        low = pl.multiple_of((offsets[tile] // 8) * 8, 8)
        alive = lax.broadcasted_iota(jnp.int32, (tile_rows, 2 * width), 0) < live[tile]
        span = pl.ds(pl.multiple_of(tile * tile_rows, tile_rows), tile_rows)
        shrink = terms_in[0, span, :].astype(jnp.float32)
        for i in range(1, terms):
            shrink = shrink + terms_in[i, span, :].astype(jnp.float32)
        shrink = shrink.astype(jnp.bfloat16)
        wide = source[pl.ds(low, tile_rows + 8), :]
        base = pltpu.roll(wide, tile_rows + 8 - offsets[tile] % 8, 0)[:tile_rows]
        expand = [
            jnp.dot(
                shrink[:, which * half : (which + 1) * half],
                ups[tile, which],
                preferred_element_type=jnp.float32,
            )
            for which in range(2)
        ]
        value = jnp.where(alive, base + jnp.concatenate(expand, axis=1), 0.0)
        out[rows] = value.astype(out.dtype).reshape(tile_rows, 2, width)

    for i in range(per_step):
        tile = t * per_step + i
        rows = slice(i * tile_rows, (i + 1) * tile_rows)
        pltpu.make_async_copy(pools[0].at[0], ups.at[tile], sems.at[tile]).wait()
        pl.when(over)(functools.partial(put, tile, held, rows))
        pl.when(jnp.logical_not(over))(functools.partial(put, tile, base, rows))


def finish(offsets, live, kind, places, totals, rest, parts, pools):
    tiles = offsets.shape[0]
    rows, columns = parts[0].shape
    tile_rows = rows // tiles
    width = totals.shape[1] // 2
    per_step = 2 if tiles % 2 == 0 else 1
    return pl.pallas_call(
        functools.partial(finish_kernel, len(pools), len(parts)),
        out_shape=jax.ShapeDtypeStruct((rows, 2, width), jnp.bfloat16),
        grid_spec=pltpu.PrefetchScalarGridSpec(
            num_scalar_prefetch=4,
            grid=(tiles // per_step,),
            in_specs=[
                pl.BlockSpec(totals.shape, lambda t, *s: (0, 0)),
                pl.BlockSpec(memory_space=pltpu.HBM),
            ]
            + [pl.BlockSpec(memory_space=pltpu.HBM)] * (len(parts) + len(pools)),
            out_specs=pl.BlockSpec((per_step * tile_rows, 2, width), lambda t, *s: (t, 0, 0)),
            scratch_shapes=[
                pltpu.VMEM((rows + tile_rows, 2 * width), jnp.float32),
                pltpu.VMEM((tiles,) + pools[0].shape[1:], pools[0].dtype),
                pltpu.VMEM((len(parts), rows, columns), parts[0].dtype),
                pltpu.SemaphoreType.DMA((tiles,)),
                pltpu.SemaphoreType.DMA((len(parts),)),
                pltpu.SemaphoreType.DMA,
            ],
        ),
        compiler_params=pltpu.CompilerParams(vmem_limit_bytes=48 << 20),
    )(offsets, live, kind, places, totals, rest, *parts, *pools)


def on_device(
    input_rows,
    key_value_weight,
    adapter_down_weight,
    adapter_up_weight,
    tile_page_index,
    tile_live_rows,
):
    groups = lax.axis_size("groups")
    ranks = lax.axis_size("dp")
    shares = lax.axis_size("tensor")
    group = lax.axis_index("groups")
    rank = lax.axis_index("dp")
    share = lax.axis_index("tensor")
    chips = ranks // 2
    chip, core = rank // 2, rank % 2
    tiles = tile_live_rows.shape[0]
    local_pages = adapter_down_weight.shape[0]
    chip_pages = 2 * local_pages
    capacity = max(2, (2 * tiles + ranks - 1) // ranks)
    most_slots = 2 * capacity
    rows, features = input_rows.shape
    tile_rows = rows // tiles
    column_width = key_value_weight.shape[2]
    half = adapter_down_weight.shape[2] // 2

    columns = 2 * column_width
    plane = groups * ranks
    part = features // plane

    line = []

    def ready(value):
        return after(value, line[-1]) if line else value

    def mark(value):
        line.append(jax.tree.leaves(value)[0])
        return value

    def wait(value):
        return mark(ready(value))

    mate_up = flip(adapter_up_weight, "dp", ranks, 1)
    mate_down = flip(adapter_down_weight, "dp", ranks, 1)
    mate_rows = flip(input_rows, "dp", ranks, 1)

    steps = [("dp", ranks, m, (rank // m) % 2) for m in bits(ranks, 2)]
    steps += [("groups", groups, m, (group // m) % 2) for m in bits(groups)]
    steps += [("dp", ranks, 1, core)]
    over_chips = len(bits(ranks, 2))
    last_step = len(steps) - 1
    spot = sum(bit << i for i, (_, _, _, bit) in enumerate(steps))
    turns = list(range(shares - 1, 0, -1))
    order = spot ^ jnp.arange(plane, dtype=jnp.int32)
    entries = [(turns[0], 0)] + [(k, i) for k in turns[1:] for i in range(chips)]
    starts = (share ^ jnp.array([k for k, _ in entries], jnp.int32)) * plane + (
        spot ^ jnp.array([i for _, i in entries], jnp.int32)
    )
    piece = lax.dynamic_slice_in_dim(
        key_value_weight, (share ^ turns[0]) * features + spot * part, part, 0
    )
    piece = mark(piece.reshape(part, columns))
    weights = {turns[0]: flip(piece, "tensor", shares, turns[0])}
    for k in turns[1:]:
        count = chips
        piece = mark(
            side_by_side(starts, ready(key_value_weight), part, entries.index((k, 0)), count)
        )[0]
        weights[k] = piece.reshape(count * part, columns)

    moving = {}

    def begin(key, step):
        axis, size, m, _ = steps[step]
        moving[key, step] = flip(weights[key], axis, size, m)

    def end(key, step):
        got = wait(moving.pop((key, step)))
        weights[key] = mark(jnp.concatenate([weights[key], got]))

    def go_on(key):
        got = wait(moving.pop((key, last_step - 1)))
        axis, size, m, _ = steps[last_step]
        gathered[key] = [weights[key], got] + [flip(v, axis, size, m) for v in (weights[key], got)]

    def get_all(key):
        gathered[key] = gathered[key][:2] + [wait(value) for value in gathered[key][2:]]
        return gathered[key]

    gathered = {}
    arrived = {}

    def lowest(k):
        return k & -k if k else shares

    def take(k, arrived):
        return [arrived.pop(k + m) for m in bits(lowest(k))]

    table = tile_page_index.reshape(chips, 2 * tiles)
    page_range = jnp.arange(ranks * local_pages, dtype=jnp.int32)
    need = jnp.any(table[:, :, None] == page_range[None, None, :], axis=1)
    need = need.reshape(chips, chips, chip_pages)
    position = jnp.cumsum(need.astype(jnp.int32), axis=2) - 1
    usual = -(-5 * most_slots // 8)
    more = -(-6 * most_slots // 8)
    cuts = [0, max(1, 2 * usual // 5), max(2, 4 * usual // 5), usual]
    firsts = [0, 2 * usual, 2 * more, 2 * most_slots]
    most_pages = jnp.max(
        jnp.where(jnp.eye(chips, dtype=jnp.bool_), 0, position[:, :, -1] + 1)
    )
    slot_range = jnp.arange(2 * most_slots, dtype=jnp.int32)
    chip_range = jnp.arange(chip_pages, dtype=jnp.int32)

    offsets = jnp.cumsum(tile_live_rows) - tile_live_rows
    live_total = jnp.sum(tile_live_rows)
    live = jnp.arange(tile_rows, dtype=jnp.int32)[None, :] < tile_live_rows[:, None]
    packed_place = offsets[:, None] + jnp.arange(tile_rows, dtype=jnp.int32)[None, :]
    packed_place = jnp.where(live, packed_place, -1).reshape(rows)
    room = -(-13 * rows // 256) * 16

    listed = []
    for offset in range(1, chips):
        wanted = need[chip ^ offset, chip]
        place = position[chip ^ offset, chip]
        listed.append(
            jnp.sum(
                jnp.where(
                    wanted[None, :] & (place[None, :] == slot_range[:, None]), chip_range[None, :], 0
                ),
                axis=1,
            )
        )
    sent_lists = []
    for offset in range(1, chips):
        halves = [
            listed[offset - 1][low:high].reshape(2, (high - low) // 2)
            for low, high in zip(firsts[:-1], firsts[1:])
        ]
        halves = jnp.concatenate(halves, axis=1)
        sent = jnp.where(core == 0, halves[0], halves[1])
        mine = ((sent // local_pages) == core).astype(jnp.int32)
        at = sent % local_pages
        sent_lists.append((at * mine, at * (1 - mine), mine))

    def locate(pages):
        owner = pages // local_pages
        entry = position[chip, owner // 2, pages % chip_pages]
        return pages % local_pages, owner, (owner // 2) ^ chip, entry

    page_lists = tile_page_index.reshape(ranks, tiles)
    at_home, owner, step, entry = locate(
        jnp.concatenate([page_lists[rank], page_lists[rank ^ 1]])
    )
    kind, places = jnp.where(owner == rank, 0, -1), at_home
    up_kind, up_places = jnp.where(owner == rank, 0, 1), at_home
    for stage in range(3):
        count = (firsts[stage + 1] - firsts[stage]) // 2
        if count == 0:
            continue
        here = (step != 0) & (entry >= firsts[stage])
        sender, at = (entry - firsts[stage]) // count, (entry - firsts[stage]) % count
        far = (sender != core).astype(jnp.int32)
        up_kind = jnp.where(here, 2 + 2 * stage + far, up_kind)
        up_places = jnp.where(here, (step - 1) * count + at, up_places)
        if stage:
            kind = jnp.where(here, (len(cuts) - 1) * (chips - 1) + stage, kind)
            places = jnp.where(here, (step - 1) * count + at, places)
        else:
            for offset in range(1, chips):
                for i in range(len(cuts) - 1):
                    chosen = here & (step == offset) & (at >= cuts[i])
                    kind = jnp.where(chosen, i * (chips - 1) + offset, kind)
                    places = jnp.where(chosen, at - cuts[i], places)
        kind = jnp.where(here & (far == 1), -1, kind)
    up_kind = up_kind[:tiles].astype(jnp.int32)
    up_places = up_places[:tiles].astype(jnp.int32)
    kind, places = kind.astype(jnp.int32), places.astype(jnp.int32)

    first, direct = turns[0], turns[-1]
    crossing = {}
    shared = {}

    def cross(i):
        for offset in range(1, chips):
            crossing[offset, i] = flip(ready(picked[offset - 1][i]), "dp", ranks, 2 * offset)

    def share_pages(i):
        shared[i] = [wait(crossing[offset, i]) for offset in range(1, chips)]

    def product(k):
        added = [wait(value) for value in take(k, arrived)]
        sent = mark(multiply(ready(aside), gathered[k], added, jnp.bfloat16))
        arrived[k] = flip(sent, "tensor", shares, lowest(k))

    def hold(k):
        arrived[k] = wait(arrived[k])

    mate_up = wait(mate_up)
    weights[first] = wait(weights[first])
    begin(first, 0)
    for k in turns[1:-1]:
        weights[k] = flip(ready(weights[k]), "tensor", shares, k)
    weights[direct] = flip(ready(weights[direct]), "tensor", shares, direct)
    mate_down = wait(mate_down)
    mate_rows = wait(mate_rows)
    picked = [
        mark(
            pick_pages(
                lists, 0, cuts, adapter_down_weight, ready(mate_down), adapter_up_weight, mate_up
            )
        )
        for lists in sent_lists
    ]
    cross(0)
    for value in (kind, places, up_kind, up_places):
        mark(value)
    for step in range(over_chips):
        end(first, step)
        begin(first, step + 1)
    packed, aside = pack(packed_place, ready(input_rows), order, part, 0, room)
    mark(aside)
    for k in turns[1:-1]:
        weights[k] = wait(weights[k])
        begin(k, last_step - 1)
    weights[direct] = wait(weights[direct])
    begin(direct, last_step - 1)
    go_on(first)
    get_all(first)
    product(first)
    cross(1)
    cross(2)
    for k in turns[1:-1]:
        go_on(k)
    share_pages(0)
    go_on(direct)
    for k in turns[1:-1]:
        get_all(k)
    values = {
        k: mark(multiply(ready(aside), gathered[k], [], jnp.float32)) for k in turns[1:-1]
    }
    hold(first)
    for k in turns[1:-1]:
        added = [wait(value) for value in take(k, arrived)]
        sent = mark(add_up([values[k]] + added, jnp.bfloat16))
        arrived[k] = flip(sent, "tensor", shares, lowest(k))
    get_all(direct)
    product(direct)
    share_pages(1)
    up_pools = [adapter_up_weight, mate_up]
    more_pools = []
    for stage in (1, 2):

        def send_more(sources):
            low, count = firsts[stage] // 2, (firsts[stage + 1] - firsts[stage]) // 2
            got = []
            for offset in range(1, chips):
                down, up = pick_pages(sent_lists[offset - 1], low, [0, count], *sources)
                got.append((flip(down, "dp", ranks, 2 * offset), flip(up, "dp", ranks, 2 * offset)))
            down = jnp.concatenate([pair[0] for pair in got])
            up = jnp.concatenate([pair[1] for pair in got])
            return down, up, flip(up, "dp", ranks, 1)

        def send_none(sources):
            own_down, _, own_up, _ = sources
            count = (chips - 1) * (firsts[stage + 1] - firsts[stage]) // 2
            down = jax.ShapeDtypeStruct((count,) + own_down.shape[1:], own_down.dtype)
            up = jax.ShapeDtypeStruct((count,) + own_up.shape[1:], own_up.dtype)
            return tuple(blank(down, up, up))

        if firsts[stage + 1] > firsts[stage]:
            near, near_up, far_up = lax.cond(
                most_pages > firsts[stage],
                send_more,
                send_none,
                (ready(adapter_down_weight), mate_down, adapter_up_weight, mate_up),
            )
            more_pools.append(near)
            up_pools += [near_up, far_up]

    near_ups = [
        flip(ready(up), "dp", ranks, 2 * (i + 1)) for i, (*_, up) in enumerate(picked)
    ]
    at = share * plane + jnp.arange(plane, dtype=jnp.int32)
    own = mark(side_by_side(at, ready(key_value_weight), part, 0, plane)[0])
    own = own.reshape(features, columns)
    share_pages(2)
    pools = [adapter_down_weight] + sum((shared[i] for i in range(3)), []) + more_pools
    shrink, mate_shrink = mark(
        tile_shrink(kind, places, ready(input_rows), mate_rows, pools, tiles)
    )
    mate_shrink = flip(mate_shrink, "dp", ranks, 1)
    parts = [mark(shrink + wait(mate_shrink))]
    parts.append(flip(parts[0], "tensor", shares, 1))
    usual_up = jnp.concatenate([wait(up) for up in near_ups])
    usual_ups = [usual_up, flip(usual_up, "dp", ranks, 1)]
    for k in turns[1:-1]:
        if k in arrived:
            hold(k)
    arrived[direct] = wait(arrived[direct])
    parts[-1] = wait(parts[-1])
    later = bits(shares, 2)
    for m in later:
        sent = sum(value.astype(jnp.float32) for value in parts).astype(jnp.bfloat16)
        parts.append(flip(mark(sent), "tensor", shares, m))
        if m != later[-1]:
            parts[-1] = wait(parts[-1])
    final = [wait(value) for value in take(0, arrived)]
    totals = mark(
        multiply(ready(packed), [own], final, jnp.float32, rows - room + tile_rows)
    )
    up_pools[2:2] = usual_ups
    parts[-1] = wait(parts[-1])

    def project_rest(operands):
        x, gathered, own = operands
        packed, aside = pack(packed_place, x, order, part, room, rows)
        arrived = {}
        for k in turns:
            sent = multiply(aside, gathered[k], take(k, arrived), jnp.bfloat16)
            arrived[k] = flip(sent, "tensor", shares, lowest(k))
        return multiply(packed, [own], take(0, arrived), jnp.float32)

    rest_shape = jax.ShapeDtypeStruct((rows - room, columns), jnp.float32)
    rest = lax.cond(
        live_total > room,
        project_rest,
        lambda operands: blank(rest_shape)[0],
        (input_rows, gathered, own),
    )
    return finish(
        offsets,
        tile_live_rows,
        up_kind,
        up_places,
        totals,
        rest,
        parts,
        up_pools,
    )


def solution(mesh):
    return jax.shard_map(
        on_device,
        mesh=mesh,
        in_specs=(
            P(("groups", "dp"), "tensor"),
            P(None, None, "tensor"),
            P("dp", "tensor", None),
            P("dp", None, None, "tensor"),
            P("groups"),
            P(("groups", "dp")),
        ),
        out_specs=P(("groups", "dp"), None, "tensor"),
        check_vma=False,
    )
```
